256 devices in a mesh: aux: 16 (over x, y), orb: 16 (over z, core).
Axes of the slice: x: 4, y: 4, z: 8, core: 2. Of those that a mesh axis runs over, the one named last changes fastest.
Arguments:
- integrals: bfloat16 [6144, 64, 256], P(('aux', 'orb')), may hold values from -0.375 to 0.375
- coefficients: bfloat16 [160, 64, 512], P('orb'), may hold values from -0.29882812 to 0.29882812
- pair_list: int32 [6144], P(('aux', 'orb')), may hold values from 0 to 159, as said below
- partial_owner: int32 [7680, 1], P(('aux', 'orb')), may hold values from 0 to 15; in each aligned block of 30 rows (0 to 29, 30 to 59, ...) at most 8 rows name the same one
- partial_slot: int32 [7680], P(('aux', 'orb')), may hold values from 0 to 15
Outputs:
- exchange_blocks: float32 [256, 4096], P(('aux', 'orb'))
The draws below stay inside these ranges and needn't reach their ends.
Inputs may be any that keep to these rules, and one draw needn't show every extreme that they name: `pair_list`: entries 4 s to 4 s + 3 of a device's 24 belong to its local block s: the first two are different blocks of the range o * 10 to (o + 1) * 10 - 1 of its own orb index o, the last two are different blocks of the range of one other orb index, and the 6 local blocks of a device use 6 different other orb indices. `partial_owner`: among the 30 partial blocks of one device no aux index is named more than 8 times, and some device names one exactly 8 times.
All inputs are finite; a program needn't handle non-finite values.
Results may differ from the reference program's by a relative error of at most 0.0039.
Values may be sent and summed in bfloat16 or wider, within the bound.
A program may use at most 64 MiB of HBM per device.

```python
import math
import jax
import jax.numpy as jnp
import numpy as np
from jax import lax

NB = 160
BS = 64
NOCC = 512
NPA = 4
LMB = 6
KB_DEV = 1
CAP = 8
NPAIR = 24
NKP = 30
NKB = 256
N_AUX = 16
N_ORB = 16
DEVICES = 256


def shuffled_rows(key, row_count, length):
    scores = jax.random.randint(key, (row_count, length), 0, 2 ** 20) * length + jnp.arange(length)[None, :]
    return jnp.argsort(scores, axis=1).astype(jnp.int32)


def draw_pair_list(key, part):
    key = jax.random.fold_in(key, 11)
    key_near, key_group, key_far = jax.random.split(key, 3)
    group_blocks = NB // N_ORB
    own_group = (jnp.arange(DEVICES) % N_ORB).astype(jnp.int32)
    slot_ids = jnp.arange(LMB)
    near_order = shuffled_rows(key_near, DEVICES, group_blocks)
    near_first = near_order[:, 2 * slot_ids % group_blocks]
    near_second = near_order[:, (2 * slot_ids + 1) % group_blocks]
    other_order = shuffled_rows(key_group, DEVICES, N_ORB - 1)[:, :LMB]
    far_group = (own_group[:, None] + 1 + other_order) % N_ORB
    far_offsets = shuffled_rows(key_far, DEVICES * LMB, group_blocks)[:, :2].reshape(DEVICES, LMB, 2)
    base_near = (own_group * group_blocks)[:, None]
    blocks_chosen = jnp.stack([base_near + near_first, base_near + near_second, far_group * group_blocks + far_offsets[:, :, 0], far_group * group_blocks + far_offsets[:, :, 1]], axis=2)
    return blocks_chosen.reshape(-1).astype(jnp.int32)


def place_ends(drawn, rng, low, high):
    extent = drawn.shape
    place = [jax.random.randint(jax.random.fold_in(rng, axis), (), 0, extent[axis]) for axis in range(len(extent))]
    drawn = drawn.at[tuple(place)].set(low)
    longest = extent.index(max(extent))
    place[longest] = (place[longest] + 1) % extent[longest]
    return drawn.at[tuple(place)].set(high)


def shard_levels(own_key, dims, pieces, least, top_value):
    def one(axis_at, blocks):
        draws = jax.random.uniform(jax.random.fold_in(jax.random.fold_in(own_key, 6), axis_at), (blocks,), jnp.float32, least / len(pieces), top_value / len(pieces))
        return jnp.repeat(jnp.exp(draws), dims[axis_at] // blocks).reshape((-1,) + (1,) * (len(dims) - axis_at - 1))

    loudness = one(*pieces[0])
    for cut in pieces[1:]:
        loudness = loudness * one(*cut)
    return loudness


def routed_block(key, own, number, rows, count, top, most, slope):
    ranking = jax.random.permutation(key, count)
    heavy_load, common = shares(count, rows * top, most, slope, True), shares(count, rows * top, most, slope, False)
    places = jnp.arange(count)

    def named(sizes, turn):
        used = int((sizes > 0).sum())
        fixed = max(1, used // 4)
        shifted = fixed + (places - fixed + turn * (used - fixed)) % max(1, count - fixed)
        return jnp.zeros((count,), jnp.int32).at[ranking[jnp.where(places < fixed, places, shifted)]].set(jnp.asarray(sizes, jnp.int32))

    sizes = jnp.where(number % 4 == 0, named(heavy_load, number // 4), named(common, number - number // 4 - 1))
    mixed = jax.random.permutation(jax.random.fold_in(own, 3), count)
    donor, taker = mixed[0:count // 2 * 2:2], mixed[1:count // 2 * 2:2]
    slack = jnp.minimum(sizes[donor] - 1, most - sizes[taker]) // 2
    slack = jnp.where((donor == ranking[0]) | (taker == ranking[0]) | (sizes[taker] == 0), 0, jnp.maximum(slack, 0))
    shifted = jax.random.randint(jax.random.fold_in(own, 4), (count // 2,), 0, 1 << 20) % (slack + 1)
    sizes = sizes.at[donor].add(-shifted).at[taker].add(shifted)
    items = jnp.searchsorted(jnp.cumsum(sizes), jnp.arange(rows * top), side="right").astype(jnp.int32)
    grid = items.reshape(top, rows).T
    grid = grid[jax.random.permutation(jax.random.fold_in(own, 1), rows)]
    turn = jax.random.randint(jax.random.fold_in(own, 2), (rows, 1), 0, top)
    return jnp.take_along_axis(grid, (jnp.arange(top)[None, :] + turn) % top, axis=1)


def shares(amount, total, bound, slope, full):
    loads = [(1 << 20) // math.isqrt(grade ** slope) + 1 for grade in range(1, amount + 1)]
    largest = bound if full else min(bound, max(-(-total // amount), total * loads[0] // sum(loads)))
    least = 1 if total - largest >= amount - 1 else 0
    holding, surplus = [largest] + [least] * (amount - 1), total - largest - least * (amount - 1)
    while surplus > 0:
        movable = [i for i in range(1, amount) if holding[i] < largest] or [i for i in range(1, amount) if holding[i] < bound]
        whole, remaining = sum([loads[i] for i in movable]), surplus
        for i in movable:
            addition = min(bound - holding[i], max(1, remaining * loads[i] // whole), surplus)
            holding[i] = holding[i] + addition
            surplus = surplus - addition
    return np.array(holding)


def gaussian(rng, dims, spread, bound, shards=(), kind=jnp.bfloat16):
    entries = spread * jax.random.normal(rng, dims, jnp.float32)
    if shards:
        entries = entries * shard_levels(rng, dims, shards, -0.22, 0.18)
    return jnp.clip(entries, -bound, bound).astype(kind)


def setup_inputs(seed: int = 0) -> dict:
    splits = jax.random.split(jax.random.key(seed), 6)
    integrals = gaussian(splits[0], (DEVICES * NPAIR, BS, BS * NPA), (4 * BS) ** -0.5, 0.375, ((0, 256),))
    coefficients = gaussian(splits[1], (NB, BS, NOCC), 0.05, 0.29882812, ((0, 16),))
    pair_list = draw_pair_list(jax.random.fold_in(splits[5], 71), 0)
    partial_owner_keys = jax.random.split(jax.random.fold_in(splits[3], 1), (DEVICES * NKP) // NKP)
    partial_owner_turns = jax.random.permutation(jax.random.fold_in(splits[3], 3), (DEVICES * NKP) // NKP)
    partial_owner = jax.vmap(lambda own, number: routed_block(jax.random.fold_in(splits[3], 2), own, number, NKP, N_AUX, 1, CAP, 2))(partial_owner_keys, partial_owner_turns).reshape((DEVICES * NKP, 1))
    partial_slot = place_ends(jax.random.randint(splits[4], (DEVICES * NKP,), 0, KB_DEV * N_ORB), jax.random.fold_in(splits[4], 1), 0, (KB_DEV * N_ORB) - 1).astype(jnp.int32)
    return dict(integrals=integrals, coefficients=coefficients, pair_list=pair_list, partial_owner=partial_owner, partial_slot=partial_slot)


def slot_pairs(count):
    table = np.array([[row_slot, col_slot] for row_slot in range(count) for col_slot in range(count) if row_slot != col_slot], dtype=np.int32)
    return table[:, 0], table[:, 1]


def reference(integrals, coefficients, pair_list, partial_owner, partial_slot):
    integral_rows = integrals.reshape(DEVICES, LMB, 4 * BS, BS * NPA)
    pair_rows = pair_list.reshape(DEVICES, NPAIR)
    target_rows = (partial_owner[:, 0] * (KB_DEV * N_ORB) + partial_slot).astype(jnp.int32).reshape(DEVICES, NKP)
    left_slots, right_slots = slot_pairs(LMB)

    def accumulate(running_sum, device_item):
        block_ints, block_pairs, block_rows = device_item
        gathered = coefficients[block_pairs].reshape(LMB, 4 * BS, NOCC)
        halfway = jnp.einsum('sla,sli->sai', block_ints.astype(jnp.float32), gathered.astype(jnp.float32))
        halfway = halfway.astype(jnp.bfloat16).astype(jnp.float32).reshape(LMB, BS, NPA, NOCC)
        products = jnp.einsum('smpi,tnpi->stmn', halfway, halfway)
        partials = products[left_slots, right_slots].reshape(NKP, BS * BS)
        return running_sum.at[block_rows].add(partials), None

    running_sum, unused = lax.scan(accumulate, jnp.zeros((NKB, BS * BS), jnp.float32), (integral_rows, pair_rows, target_rows))
    return running_sum
```

```python
import functools

import jax
import jax.numpy as jnp
from jax import lax
from jax.experimental import pallas as pl
from jax.experimental.pallas import tpu as pltpu
from jax.sharding import PartitionSpec as P

MESH = pl.DeviceIdType.MESH
F32, BF16, I32 = jnp.float32, jnp.bfloat16, jnp.int32


def kernel(
    dims,
    ints_ref,
    coef_ref,
    pairs_ref,
    owner_ref,
    slot_ref,
    out_ref,
    gbuf,
    cbuf,
    zbuf,
    msgs,
    idsm,
    packed,
    sel,
    gt,
    hcat,
    xbuf,
    xsend,
    xrecv,
    onehot,
    dsend,
    drecv,
    fsend,
    frecv,
    load_sem,
    zs_sem,
    zr_sem,
    ws_sem,
    wr_sem,
    is_sem,
    ir_sem,
    ps_sem,
    pr_sem,
    xs_sem,
    xr_sem,
    ds_sem,
    dr_sem,
    fs_sem,
    fr_sem,
):
    na, no, lmb, bs, nocc, naux, per = dims
    nz = no // 2
    nic = nocc // 128
    mp = bs // na // 2
    half = lmb // 2
    width = na * 16
    rows = na * no
    el = mp * 128
    a = lax.axis_index("aux")
    o = lax.axis_index("orb")
    z, c = o // 2, o % 2
    sib = o + 1 - 2 * c
    lg = pl.multiple_of((a // nic) * 16, 16)
    lane0 = pl.multiple_of((a % nic) * 128, 128)
    ic = a % nic

    load_c = pltpu.make_async_copy(coef_ref, cbuf, load_sem.at[0])
    load_g = pltpu.make_async_copy(ints_ref, gbuf, load_sem.at[1])
    load_c.start()
    load_g.start()

    barrier = pltpu.get_barrier_semaphore()

    def greet_aux(i, _):
        pl.semaphore_signal(barrier, inc=1, device_id=((a + i) % na, o), device_id_type=MESH)
        return 0

    def greet_orb(i, _):
        pl.semaphore_signal(barrier, inc=1, device_id=(a, (o + i) % no), device_id_type=MESH)
        return 0

    lax.fori_loop(1, no, greet_orb, 0)
    lax.fori_loop(1, na, greet_aux, 0)

    row_at = lax.broadcasted_iota(I32, (8, width), 0)
    lane_at = lax.broadcasted_iota(I32, (8, width), 1)
    note = jnp.zeros((8, width), I32)
    for s in range(lmb):
        for t in range(lmb):
            if s != t:
                j = s * (lmb - 1) + t - (1 if t > s else 0)
                place = slot_ref[j] * na + owner_ref[j] + 1
                here = (row_at == t) & ((lane_at == a * 16 + s) | (lane_at == a * 16 + 8 + s))
                note = jnp.where(here, place, note)
    for j in range(4 * lmb):
        note = jnp.where((row_at == lmb) & (lane_at == j), pairs_ref[j], note)
    msgs[a] = note

    pl.semaphore_wait(barrier, na + no - 2)
    load_c.wait()

    tiles = cbuf.at[:, pl.ds(lg, 16), pl.ds(lane0, 128)]
    mine = pltpu.make_async_copy(tiles, zbuf.at[pl.ds(o * per, per)], load_sem.at[2])

    def z_copy(i):
        return pltpu.make_async_remote_copy(
            src_ref=tiles,
            dst_ref=zbuf.at[pl.ds(o * per, per)],
            send_sem=zs_sem.at[i],
            recv_sem=zr_sem.at[z],
            device_id=(a, ((z + i) % nz) * 2 + c),
            device_id_type=MESH,
        )

    def z_arrival(i):
        src = (z + i) % nz
        part = zbuf.at[pl.ds((src * 2 + c) * per, per)]
        return pltpu.make_async_remote_copy(
            src_ref=part,
            dst_ref=part,
            send_sem=zs_sem.at[i],
            recv_sem=zr_sem.at[src],
            device_id=(a, sib),
            device_id_type=MESH,
        )

    def own_swap():
        return pltpu.make_async_remote_copy(
            src_ref=tiles,
            dst_ref=zbuf.at[pl.ds(o * per, per)],
            send_sem=ws_sem.at[z],
            recv_sem=wr_sem.at[z],
            device_id=(a, sib),
            device_id_type=MESH,
        )

    def swap_copy(i):
        src = (z + i) % nz
        part = zbuf.at[pl.ds((src * 2 + c) * per, per)]
        return pltpu.make_async_remote_copy(
            src_ref=part,
            dst_ref=part,
            send_sem=ws_sem.at[src],
            recv_sem=wr_sem.at[src],
            device_id=(a, sib),
            device_id_type=MESH,
        )

    def swap_arrival(i):
        src = (z + i) % nz
        part = zbuf.at[pl.ds((src * 2 + 1 - c) * per, per)]
        return pltpu.make_async_remote_copy(
            src_ref=part,
            dst_ref=part,
            send_sem=ws_sem.at[src],
            recv_sem=wr_sem.at[src],
            device_id=(a, sib),
            device_id_type=MESH,
        )

    def start_z(i, _):
        z_copy(i).start()
        return 0

    lax.fori_loop(1, nz, start_z, 0)
    own_swap().start()
    mine.start()

    def id_copy(i):
        return pltpu.make_async_remote_copy(
            src_ref=msgs.at[a],
            dst_ref=msgs.at[a],
            send_sem=is_sem.at[i],
            recv_sem=ir_sem.at[a],
            device_id=((a + i) % na, o),
            device_id_type=MESH,
        )

    def id_arrival(i):
        src = (a + i) % na
        return pltpu.make_async_remote_copy(
            src_ref=msgs.at[src],
            dst_ref=msgs.at[src],
            send_sem=is_sem.at[i],
            recv_sem=ir_sem.at[src],
            device_id=(src, o),
            device_id_type=MESH,
        )

    def start_ids(i, _):
        id_copy(i).start()
        return 0

    lax.fori_loop(1, na, start_ids, 0)

    for s in range(lmb):
        for k in range(2):
            block = cbuf[lax.rem(pairs_ref[4 * s + k], per)]
            for i in range(nic):
                sel[i, s, k] = block[:, i * 128 : (i + 1) * 128]

    load_g.wait()
    height = bs * naux
    r_at = lax.broadcasted_iota(I32, (height, height), 0)
    c_at = lax.broadcasted_iota(I32, (height, height), 1)
    turn = (c_at == (r_at % bs) * naux + r_at // bs).astype(F32).astype(BF16)
    for s in range(lmb):
        block = gbuf[4 * s : 4 * s + 4].reshape(4 * bs, height)
        gt[s] = lax.dot_general(turn, block, (((1,), (1,)), ((), ())), preferred_element_type=F32).astype(BF16)
    xbuf[...] = jnp.zeros_like(xbuf)

    def wait_ids(i, _):
        id_arrival(i).wait_recv()
        return 0

    lax.fori_loop(1, na, wait_ids, 0)
    to_scalar = pltpu.make_async_copy(msgs.at[:, :, pl.ds(0, min(width, 128))], idsm, load_sem.at[3])
    to_scalar.start()

    ids = msgs[0]
    for src in range(1, na):
        ids = ids + msgs[src]
    r_at = lax.broadcasted_iota(I32, (rows, width), 0) + 1
    l_at = (lax.broadcasted_iota(I32, (rows, width), 1) // 8) % 2
    for h in range(2):
        for tp in range(half):
            hit = r_at == ids[2 * tp + h : 2 * tp + h + 1, :]
            for m2 in range(2):
                onehot[pl.ds((m2 * 2 + h) * rows, rows), pl.ds(tp * width, width)] = (
                    jnp.where(hit & (l_at == m2), 1.0, 0.0).astype(BF16)
                )
    to_scalar.wait()

    def forward(i, _):
        z_arrival(i).wait_recv()
        swap_copy(i).start()
        return 0

    lax.fori_loop(1, nz, forward, 0)
    mine.wait()

    def wait_swap(i, _):
        swap_arrival(i).wait_recv()
        return 0

    lax.fori_loop(0, nz, wait_swap, 0)

    def pack_copy(i):
        to = (a + i) % na
        return pltpu.make_async_remote_copy(
            src_ref=packed.at[to],
            dst_ref=sel.at[ic, :, pl.ds(2, 2), pl.ds(lg, 16), :],
            send_sem=ps_sem.at[i],
            recv_sem=pr_sem.at[a],
            device_id=(to, o),
            device_id_type=MESH,
        )

    def pack_arrival(i):
        src = (a + i) % na
        return pltpu.make_async_remote_copy(
            src_ref=packed.at[src],
            dst_ref=sel.at[src % nic, :, pl.ds(2, 2), pl.ds(pl.multiple_of((src // nic) * 16, 16), 16), :],
            send_sem=ps_sem.at[i],
            recv_sem=pr_sem.at[src],
            device_id=(src, o),
            device_id_type=MESH,
        )

    def pack(i, _):
        to = (a + i) % na
        for s in range(lmb):
            for k in range(2):
                packed[to, s, k] = zbuf[idsm[to, lmb, 4 * s + 2 + k]]
        pack_copy(i).start()
        return 0

    lax.fori_loop(1, na, pack, 0)
    for s in range(lmb):
        for k in range(2):
            sel[ic, s, 2 + k, pl.ds(lg, 16), :] = zbuf[pairs_ref[4 * s + 2 + k]]

    def wait_pack(i, _):
        pack_arrival(i).wait_recv()
        return 0

    lax.fori_loop(1, na, wait_pack, 0)

    for s in range(lmb):
        block = jnp.concatenate([sel[i, s].reshape(4 * bs, 128) for i in range(nic)], axis=1)
        halfway = jnp.dot(gt[s], block, preferred_element_type=F32).astype(BF16)
        for p in range(naux):
            hcat[pl.ds(s * bs, bs), pl.ds(p * nocc, nocc)] = halfway[p * bs : (p + 1) * bs]

    whole = hcat[...]
    for s in range(lmb):
        part = lax.dot_general(
            hcat[pl.ds(s * bs, bs), :], whole, (((1,), (1,)), ((), ())), preferred_element_type=F32
        )
        for tp in range(half):
            xbuf[tp, pl.ds(s, bs, stride=8), :] = part[:, tp * 128 : (tp + 1) * 128]

    def x_copy(i):
        to = (a + i) % na
        return pltpu.make_async_remote_copy(
            src_ref=xsend.at[to],
            dst_ref=xrecv.at[:, a],
            send_sem=xs_sem.at[i],
            recv_sem=xr_sem.at[a],
            device_id=(to, o),
            device_id_type=MESH,
        )

    def x_arrival(i):
        src = (a + i) % na
        return pltpu.make_async_remote_copy(
            src_ref=xsend.at[src],
            dst_ref=xrecv.at[:, src],
            send_sem=xs_sem.at[i],
            recv_sem=xr_sem.at[src],
            device_id=(src, o),
            device_id_type=MESH,
        )

    def x_rows(e, q):
        at = pl.ds(pl.multiple_of((e * mp + q) * 16, 16), 16)
        return jnp.concatenate([xbuf[tp, at, :] for tp in range(half)], axis=1).astype(BF16)

    def send_x(i, _):
        to = (a + i) % na
        for q in range(mp):
            xsend[to, q] = x_rows(to, q)
        x_copy(i).start()
        return 0

    lax.fori_loop(1, na, send_x, 0)
    for q in range(mp):
        xrecv[q, a] = x_rows(a, q)

    def wait_x(i, _):
        x_arrival(i).wait_recv()
        return 0

    lax.fori_loop(1, na, wait_x, 0)

    right = [
        jnp.concatenate(
            [xrecv[q, :, :, pl.ds(tp * 128, 128)].reshape(width, 128) for q in range(mp)], axis=1
        )
        for tp in range(half)
    ]

    def product(block):
        total = None
        for tp in range(half):
            term = jnp.dot(
                onehot[pl.ds(block * rows, rows), pl.ds(tp * width, width)], right[tp], preferred_element_type=F32
            )
            total = term if total is None else total + term
        return total

    z00, z01, z10, z11 = product(0), product(1), product(2), product(3)
    low = lax.broadcasted_iota(I32, (rows, 128), 1) < 64
    for q in range(mp):
        at = slice(q * 128, (q + 1) * 128)
        first = z00[:, at] + pltpu.roll(z01[:, at], 64, 1)
        second = pltpu.roll(z10[:, at], 64, 1) + z11[:, at]
        dense = jnp.where(low, first, second).astype(BF16)
        dsend[:, :, pl.ds(q * 128, 128)] = dense.reshape(no, na, 128)

    def d_copy(i):
        to = (o + i) % no
        return pltpu.make_async_remote_copy(
            src_ref=dsend.at[to],
            dst_ref=drecv.at[o],
            send_sem=ds_sem.at[i],
            recv_sem=dr_sem.at[o],
            device_id=(a, to),
            device_id_type=MESH,
        )

    def d_arrival(i):
        src = (o + i) % no
        return pltpu.make_async_remote_copy(
            src_ref=dsend.at[src],
            dst_ref=drecv.at[src],
            send_sem=ds_sem.at[i],
            recv_sem=dr_sem.at[src],
            device_id=(a, src),
            device_id_type=MESH,
        )

    def send_d(i, _):
        d_copy(i).start()
        return 0

    lax.fori_loop(1, no, send_d, 0)
    drecv[o] = dsend[o]

    def wait_d(i, _):
        d_arrival(i).wait_recv()
        return 0

    lax.fori_loop(1, no, wait_d, 0)

    total = drecv[0].astype(F32)
    for src in range(1, no):
        total = total + drecv[src].astype(F32)
    for r in range(na):
        fsend[r] = total[r : r + 1, :]

    def f_copy(i):
        to = (a + i) % na
        return pltpu.make_async_remote_copy(
            src_ref=fsend.at[to],
            dst_ref=frecv.at[a],
            send_sem=fs_sem.at[i],
            recv_sem=fr_sem.at[a],
            device_id=(to, o),
            device_id_type=MESH,
        )

    def f_arrival(i):
        src = (a + i) % na
        return pltpu.make_async_remote_copy(
            src_ref=fsend.at[src],
            dst_ref=frecv.at[src],
            send_sem=fs_sem.at[i],
            recv_sem=fr_sem.at[src],
            device_id=(src, o),
            device_id_type=MESH,
        )

    def send_f(i, _):
        f_copy(i).start()
        return 0

    lax.fori_loop(1, na, send_f, 0)
    frecv[a] = fsend[a]

    def settle_aux(i, _):
        id_copy(i).wait_send()
        pack_copy(i).wait_send()
        x_copy(i).wait_send()
        return 0

    def settle_z(i, _):
        z_copy(i).wait_send()
        swap_copy(i).wait_send()
        return 0

    def settle_d(i, _):
        d_copy(i).wait_send()
        return 0

    lax.fori_loop(1, na, settle_aux, 0)
    lax.fori_loop(1, nz, settle_z, 0)
    own_swap().wait_send()
    lax.fori_loop(1, no, settle_d, 0)

    def wait_f(i, _):
        f_arrival(i).wait_recv()
        f_copy(i).wait_send()
        return 0

    lax.fori_loop(1, na, wait_f, 0)
    for e in range(na):
        out_ref[:, pl.ds(e * el, el)] = frecv[e]


def shards(integrals, coefficients, pair_list, partial_owner, partial_slot):
    na, no = lax.axis_size("aux"), lax.axis_size("orb")
    per, bs, nocc = coefficients.shape
    lmb = pair_list.shape[0] // 4
    naux = integrals.shape[2] // bs
    mp = bs // na // 2
    width = na * 16
    rows = na * no
    el = mp * 128
    nz = no // 2
    dims = (na, no, lmb, bs, nocc, naux, per)
    dma = pltpu.SemaphoreType.DMA
    vmem = pltpu.VMEM
    any_spec = pl.BlockSpec(memory_space=pltpu.HBM)
    smem_spec = pl.BlockSpec(memory_space=pltpu.SMEM)
    return pl.pallas_call(
        functools.partial(kernel, dims),
        out_shape=jax.ShapeDtypeStruct((1, bs * bs), F32),
        in_specs=[any_spec, any_spec, smem_spec, smem_spec, smem_spec],
        out_specs=pl.BlockSpec(memory_space=pltpu.VMEM),
        scratch_shapes=[
            vmem(integrals.shape, BF16),
            vmem(coefficients.shape, BF16),
            vmem((no * per, 16, 128), BF16),
            vmem((na, 8, width), I32),
            pltpu.SMEM((na, 8, min(width, 128)), I32),
            vmem((na, lmb, 2, 16, 128), BF16),
            vmem((nocc // 128, lmb, 4, bs, 128), BF16),
            vmem((lmb, bs * naux, 4 * bs), BF16),
            vmem((lmb * bs, naux * nocc), BF16),
            vmem((lmb // 2, bs * 8, 128), F32),
            vmem((na, mp, 16, lmb * bs), BF16),
            vmem((mp, na, 16, lmb * bs), BF16),
            vmem((4 * rows, lmb // 2 * width), BF16),
            vmem((no, na, el), BF16),
            vmem((no, na, el), BF16),
            vmem((na, 1, el), F32),
            vmem((na, 1, el), F32),
            dma((4,)),
            dma((nz,)),
            dma((nz,)),
            dma((nz,)),
            dma((nz,)),
            dma((na,)),
            dma((na,)),
            dma((na,)),
            dma((na,)),
            dma((na,)),
            dma((na,)),
            dma((no,)),
            dma((no,)),
            dma((na,)),
            dma((na,)),
        ],
        compiler_params=pltpu.CompilerParams(
            collective_id=0, has_side_effects=True, vmem_limit_bytes=40 * 2**20
        ),
    )(integrals, coefficients, pair_list, partial_owner.reshape(-1), partial_slot)


def solution(mesh):
    in_specs = (
        P(("aux", "orb"), None, None),
        P("orb", None, None),
        P(("aux", "orb")),
        P(("aux", "orb"), None),
        P(("aux", "orb")),
    )
    out_specs = P(("aux", "orb"), None)
    return jax.shard_map(shards, mesh=mesh, in_specs=in_specs, out_specs=out_specs, check_vma=False)
```

```python
import functools
import math

import jax
import jax.numpy as jnp
from jax import lax
from jax.experimental import pallas as pl
from jax.experimental.pallas import tpu as pltpu
from jax.sharding import PartitionSpec as P

MESH = pl.DeviceIdType.MESH
F32, BF16, I32 = jnp.float32, jnp.bfloat16, jnp.int32


def kernel(
    dims,
    ints_ref,
    coef_ref,
    pairs_hbm,
    owner_hbm,
    slot_hbm,
    out_ref,
    pairs_ref,
    owner_ref,
    slot_ref,
    gbuf,
    cbuf,
    tiles,
    zbuf_a,
    zbuf_b,
    msgs,
    idsm,
    packed,
    near,
    far,
    gt,
    hcat,
    xbuf,
    xsend,
    xrecv,
    onehot,
    dsend,
    drecv,
    fsend,
    frecv,
    load_sem,
    send_sem,
    recv_sem,
):
    na, no, lmb, bs, nocc, naux, per = dims
    side = math.isqrt(na)
    nz = no // 2
    nic = nocc // 128
    mp = bs // na // 2
    half = lmb // 2
    width = na * 16
    rows = na * no
    el = mp * 128
    a = lax.axis_index("aux")
    o = lax.axis_index("orb")
    x, y = a // side, a % side
    z, c = o // 2, o % 2
    sib = o + 1 - 2 * c
    lg = pl.multiple_of((a // nic) * 16, 16)
    lane0 = pl.multiple_of((a % nic) * 128, 128)
    own = pl.ds(o * per, per)
    zbuf = (zbuf_a, zbuf_b)

    def plane_peer(i):
        turn = na // 2 + side // 2
        j = jnp.where(i < na - turn, i + turn, i - (na - turn) + 1)
        return ((x + j // side) % side) * side + (y + j % side) % side

    z_order = sorted(range(1, nz), key=lambda i: -min(i, nz - i))
    o_order = sorted(range(1, no), key=lambda i: -min(i, no - i))

    barrier = pltpu.get_barrier_semaphore()
    for i in o_order:
        pl.semaphore_signal(barrier, inc=1, device_id=(a, (o + i) % no), device_id_type=MESH)

    def greet(i, _):
        pl.semaphore_signal(barrier, inc=1, device_id=(plane_peer(i), o), device_id_type=MESH)
        return 0

    lax.fori_loop(0, na - 1, greet, 0)

    load_t = pltpu.make_async_copy(coef_ref.at[:, pl.ds(lg, 16), pl.ds(lane0, 128)], tiles, load_sem.at[2])
    load_c = pltpu.make_async_copy(coef_ref, cbuf, load_sem.at[0])
    load_g = pltpu.make_async_copy(ints_ref, gbuf, load_sem.at[1])
    scalars = [
        pltpu.make_async_copy(pairs_hbm, pairs_ref, load_sem.at[4]),
        pltpu.make_async_copy(owner_hbm, owner_ref, load_sem.at[5]),
        pltpu.make_async_copy(slot_hbm, slot_ref, load_sem.at[6]),
    ]
    load_t.start()
    for copy in scalars:
        copy.start()
    load_c.start()
    load_g.start()

    def remote(src, dst, stage, device):
        return pltpu.make_async_remote_copy(
            src_ref=src,
            dst_ref=dst,
            send_sem=send_sem.at[stage],
            recv_sem=recv_sem.at[stage],
            device_id=device,
            device_id_type=MESH,
        )

    def all_of(part, stage):
        return remote(part, part, stage, (a, sib))

    za, zb, wa, wb, ids_at, pa, pb, xs, ds, fs = range(10)

    load_t.wait()
    zbuf_a[own] = tiles[:, 0:8, :]
    zbuf_b[own] = tiles[:, 8:16, :]
    for copy in scalars:
        copy.wait()

    row_at = lax.broadcasted_iota(I32, (8, width), 0)
    lane_at = lax.broadcasted_iota(I32, (8, width), 1)
    note = jnp.zeros((8, width), I32)
    for s in range(lmb):
        for t in range(lmb):
            if s != t:
                j = s * (lmb - 1) + t - (1 if t > s else 0)
                place = slot_ref[j] * na + owner_ref[j] + 1
                here = (row_at == t) & ((lane_at == a * 16 + s) | (lane_at == a * 16 + 8 + s))
                note = jnp.where(here, place, note)
    for j in range(4 * lmb):
        if j % 4 >= 2:
            note = jnp.where((row_at == lmb) & (lane_at == j), pairs_ref[j], note)
    msgs[a] = note

    pl.semaphore_wait(barrier, na + no - 2)

    def start_z(h, stage):
        for i in z_order:
            remote(zbuf[h].at[own], zbuf[h].at[own], stage, (a, ((z + i) % nz) * 2 + c)).start()

    start_z(0, za)

    def start_ids(i, _):
        remote(msgs.at[a], msgs.at[a], ids_at, (plane_peer(i), o)).start()
        return 0

    lax.fori_loop(0, na - 1, start_ids, 0)
    start_z(1, zb)

    load_g.wait()
    height = bs * naux
    r_at = lax.broadcasted_iota(I32, (height, height), 0)
    c_at = lax.broadcasted_iota(I32, (height, height), 1)
    turn = (c_at == (r_at % bs) * naux + r_at // bs).astype(F32).astype(BF16)
    j = c_at - 2 * bs
    source = 2 * bs + (j // 8 % 2) * bs + (j // 16 % (bs // 16)) * 16 + (j // bs) * 8 + j % 8
    order = (r_at == jnp.where(c_at < 2 * bs, c_at, source)).astype(F32).astype(BF16)
    for s in range(lmb):
        block = gbuf[4 * s : 4 * s + 4].reshape(4 * bs, height)
        turned = lax.dot_general(turn, block, (((1,), (1,)), ((), ())), preferred_element_type=F32).astype(BF16)
        gt[s] = jnp.dot(turned, order, preferred_element_type=F32).astype(BF16)

    load_c.wait()
    for s in range(lmb):
        for k in range(2):
            near[s, pl.ds(k * bs, bs), :] = cbuf[lax.rem(pairs_ref[4 * s + k], per)]
    xbuf[...] = jnp.zeros_like(xbuf)

    all_of(msgs.at[pl.ds(0, na - 1)], ids_at).wait_recv()
    to_scalar = pltpu.make_async_copy(msgs.at[:, :, pl.ds(0, min(width, 128))], idsm, load_sem.at[3])
    to_scalar.start()

    ids = msgs[0]
    for src in range(1, na):
        ids = ids + msgs[src]
    to_scalar.wait()

    def swap(h, z_stage, w_stage):
        all_of(zbuf[h].at[pl.ds(0, (nz - 1) * per)], z_stage).wait_recv()
        for i in range(nz):
            part = zbuf[h].at[pl.ds((2 * i + c) * per, per)]
            remote(part, part, w_stage, (a, sib)).start()

    def pair(h, to, s):
        return jnp.concatenate(
            [zbuf[h][idsm[to, lmb, 4 * s + 2]], zbuf[h][idsm[to, lmb, 4 * s + 3]]], axis=0
        )

    def exchange(h, w_stage, p_stage):
        all_of(zbuf[h].at[pl.ds(0, nz * per)], w_stage).wait_recv()

        def pack(i, _):
            to = plane_peer(i)
            for s in range(lmb):
                packed[h, to, s] = pair(h, to, s)
            remote(packed.at[h, to], far.at[h, a], p_stage, (to, o)).start()
            return 0

        lax.fori_loop(0, na - 1, pack, 0)
        for s in range(lmb):
            far[h, a, s] = pair(h, a, s)

    swap(0, za, wa)
    exchange(0, wa, pa)
    swap(1, zb, wb)
    exchange(1, wb, pb)

    r_at = lax.broadcasted_iota(I32, (rows, width), 0) + 1
    l_at = (lax.broadcasted_iota(I32, (rows, width), 1) // 8) % 2
    for h in range(2):
        for tp in range(half):
            hit = r_at == ids[2 * tp + h : 2 * tp + h + 1, :]
            for m2 in range(2):
                onehot[pl.ds((m2 * 2 + h) * rows, rows), pl.ds(tp * width, width)] = (
                    jnp.where(hit & (l_at == m2), 1.0, 0.0).astype(BF16)
                )

    all_of(far.at[0, pl.ds(0, na - 1)], pa).wait_recv()
    all_of(far.at[1, pl.ds(0, na - 1)], pb).wait_recv()

    for s in range(lmb):
        there = [
            jnp.concatenate([far[h, g * nic + i, s] for h in range(2) for g in range(bs // 16)], axis=0)
            for i in range(nic)
        ]
        block = jnp.concatenate([near[s], jnp.concatenate(there, axis=1)], axis=0)
        halfway = jnp.dot(gt[s], block, preferred_element_type=F32).astype(BF16)
        for p in range(naux):
            hcat[pl.ds(s * bs, bs), pl.ds(p * nocc, nocc)] = halfway[p * bs : (p + 1) * bs]

    whole = hcat[...]
    products = lax.dot_general(whole, whole, (((1,), (1,)), ((), ())), preferred_element_type=F32)
    for s in range(lmb):
        for tp in range(half):
            xbuf[tp, pl.ds(s, bs, stride=8), :] = products[s * bs : (s + 1) * bs, tp * 128 : (tp + 1) * 128]

    def x_rows(e, q):
        at = pl.ds(pl.multiple_of((e * mp + q) * 16, 16), 16)
        return jnp.concatenate([xbuf[tp, at, :] for tp in range(half)], axis=1).astype(BF16)

    def send_x(i, _):
        to = plane_peer(i)
        for q in range(mp):
            xsend[to, q] = x_rows(to, q)
        remote(xsend.at[to], xrecv.at[a], xs, (to, o)).start()
        return 0

    lax.fori_loop(0, na - 1, send_x, 0)
    for q in range(mp):
        xrecv[a, q] = x_rows(a, q)
    all_of(xrecv.at[pl.ds(0, na - 1)], xs).wait_recv()

    right = [
        jnp.concatenate(
            [xrecv[:, q, :, pl.ds(tp * 128, 128)].reshape(width, 128) for q in range(mp)], axis=1
        )
        for tp in range(half)
    ]

    def product(block):
        total = None
        for tp in range(half):
            term = jnp.dot(
                onehot[pl.ds(block * rows, rows), pl.ds(tp * width, width)], right[tp], preferred_element_type=F32
            )
            total = term if total is None else total + term
        return total

    z00, z01, z10, z11 = product(0), product(1), product(2), product(3)
    low = lax.broadcasted_iota(I32, (rows, 128), 1) < 64
    for q in range(mp):
        at = slice(q * 128, (q + 1) * 128)
        first = z00[:, at] + pltpu.roll(z01[:, at], 64, 1)
        second = pltpu.roll(z10[:, at], 64, 1) + z11[:, at]
        dense = jnp.where(low, first, second).astype(BF16)
        dsend[:, :, pl.ds(q * 128, 128)] = dense.reshape(no, na, 128)

    for i in o_order:
        to = (o + i) % no
        remote(dsend.at[to], drecv.at[o], ds, (a, to)).start()
    drecv[o] = dsend[o]
    all_of(drecv.at[pl.ds(0, no - 1)], ds).wait_recv()

    total = drecv[0].astype(F32)
    for src in range(1, no):
        total = total + drecv[src].astype(F32)
    for r in range(na):
        fsend[r] = total[r : r + 1, :]

    def send_f(i, _):
        to = plane_peer(i)
        remote(fsend.at[to], frecv.at[a], fs, (to, o)).start()
        return 0

    lax.fori_loop(0, na - 1, send_f, 0)
    frecv[a] = fsend[a]

    for h, (z_stage, w_stage, p_stage) in enumerate(((za, wa, pa), (zb, wb, pb))):
        all_of(zbuf[h].at[pl.ds(0, (nz - 1) * per)], z_stage).wait_send()
        all_of(zbuf[h].at[pl.ds(0, nz * per)], w_stage).wait_send()
        all_of(packed.at[h, pl.ds(0, na - 1)], p_stage).wait_send()
    all_of(msgs.at[pl.ds(0, na - 1)], ids_at).wait_send()
    all_of(xsend.at[pl.ds(0, na - 1)], xs).wait_send()
    all_of(dsend.at[pl.ds(0, no - 1)], ds).wait_send()
    all_of(frecv.at[pl.ds(0, na - 1)], fs).wait_recv()
    all_of(fsend.at[pl.ds(0, na - 1)], fs).wait_send()
    for e in range(na):
        out_ref[:, pl.ds(e * el, el)] = frecv[e]


def shards(integrals, coefficients, pair_list, partial_owner, partial_slot):
    na, no = lax.axis_size("aux"), lax.axis_size("orb")
    per, bs, nocc = coefficients.shape
    lmb = pair_list.shape[0] // 4
    naux = integrals.shape[2] // bs
    mp = bs // na // 2
    width = na * 16
    rows = na * no
    el = mp * 128
    dims = (na, no, lmb, bs, nocc, naux, per)
    dma = pltpu.SemaphoreType.DMA
    vmem = pltpu.VMEM
    any_spec = pl.BlockSpec(memory_space=pltpu.HBM)
    return pl.pallas_call(
        functools.partial(kernel, dims),
        out_shape=jax.ShapeDtypeStruct((1, bs * bs), F32),
        in_specs=[any_spec] * 5,
        out_specs=pl.BlockSpec(memory_space=pltpu.VMEM),
        scratch_shapes=[
            pltpu.SMEM(pair_list.shape, I32),
            pltpu.SMEM(partial_slot.shape, I32),
            pltpu.SMEM(partial_slot.shape, I32),
            vmem(integrals.shape, BF16),
            vmem(coefficients.shape, BF16),
            vmem((per, 16, 128), BF16),
            vmem((no * per, 8, 128), BF16),
            vmem((no * per, 8, 128), BF16),
            vmem((na, 8, width), I32),
            pltpu.SMEM((na, 8, min(width, 128)), I32),
            vmem((2, na, lmb, 16, 128), BF16),
            vmem((lmb, 2 * bs, nocc), BF16),
            vmem((2, na, lmb, 16, 128), BF16),
            vmem((lmb, bs * naux, 4 * bs), BF16),
            vmem((lmb * bs, naux * nocc), BF16),
            vmem((lmb // 2, bs * 8, 128), F32),
            vmem((na, mp, 16, lmb * bs), BF16),
            vmem((na, mp, 16, lmb * bs), BF16),
            vmem((4 * rows, lmb // 2 * width), BF16),
            vmem((no, na, el), BF16),
            vmem((no, na, el), BF16),
            vmem((na, 1, el), F32),
            vmem((na, 1, el), F32),
            dma((7,)),
            dma((10,)),
            dma((10,)),
        ],
        compiler_params=pltpu.CompilerParams(
            collective_id=0, has_side_effects=True, vmem_limit_bytes=60 * 2**20
        ),
    )(integrals, coefficients, pair_list, partial_owner.reshape(-1), partial_slot)


def solution(mesh):
    in_specs = (
        P(("aux", "orb"), None, None),
        P("orb", None, None),
        P(("aux", "orb")),
        P(("aux", "orb"), None),
        P(("aux", "orb")),
    )
    out_specs = P(("aux", "orb"), None)
    return jax.shard_map(shards, mesh=mesh, in_specs=in_specs, out_specs=out_specs, check_vma=False)
```

```python
import functools
import math

import jax
import jax.numpy as jnp
from jax import lax
from jax.experimental import pallas as pl
from jax.experimental.pallas import tpu as pltpu
from jax.sharding import PartitionSpec as P

MESH = pl.DeviceIdType.MESH
F32, BF16, I32 = jnp.float32, jnp.bfloat16, jnp.int32


def block_places(lmb):
    chunks = (lmb - 2) // 2
    places = [[[None, None] for _ in range(8)] for _ in range(chunks)]
    for chunk in range(chunks):
        for s in range(lmb):
            for h in range(2):
                places[chunk][s][h] = (s, (s + 2 * chunk + 1 + h) % lmb)
    for s in range(lmb):
        row, h = divmod(s, 2)
        places[row // 2][lmb + row % 2][h] = (s, (s + lmb - 1) % lmb)
    return places


def kernel(
    dims,
    ints_ref,
    coef_ref,
    pairs_hbm,
    owner_hbm,
    slot_hbm,
    out_ref,
    pairs_ref,
    owner_ref,
    slot_ref,
    gbuf,
    cbuf,
    tiles,
    zbuf_a,
    zbuf_b,
    msgs,
    asked,
    idsm,
    packed,
    near,
    far,
    gt,
    hcat,
    xbuf,
    xsend,
    xrecv,
    onehot,
    dsend,
    drecv,
    fsend,
    frecv,
    load_sem,
    send_sem,
    recv_sem,
):
    na, no, lmb, bs, nocc, naux, per = dims
    side = math.isqrt(na)
    nz = no // 2
    nic = nocc // 128
    mp = bs // na // 2
    chunks = (lmb - 2) // 2
    places = block_places(lmb)
    width = na * 16
    rows = na * no
    el = mp * 128
    a = lax.axis_index("aux")
    o = lax.axis_index("orb")
    x, y = a // side, a % side
    z, c = o // 2, o % 2
    sib = o + 1 - 2 * c
    lg = pl.multiple_of((a // nic) * 16, 16)
    lane0 = pl.multiple_of((a % nic) * 128, 128)
    own = pl.ds(o * per, per)
    zbuf = (zbuf_a, zbuf_b)

    def plane_peer(i):
        turn = na // 2 + side // 2
        j = jnp.where(i < na - turn, i + turn, i - (na - turn) + 1)
        return ((x + j // side) % side) * side + (y + j % side) % side

    z_order = sorted(range(1, nz), key=lambda i: -min(i, nz - i))
    o_order = sorted(range(1, no), key=lambda i: -min(i, no - i))

    barrier = pltpu.get_barrier_semaphore()
    for i in o_order:
        pl.semaphore_signal(barrier, inc=1, device_id=(a, (o + i) % no), device_id_type=MESH)

    def greet(i, _):
        pl.semaphore_signal(barrier, inc=1, device_id=(plane_peer(i), o), device_id_type=MESH)
        return 0

    lax.fori_loop(0, na - 1, greet, 0)

    load_t = pltpu.make_async_copy(coef_ref.at[:, pl.ds(lg, 16), pl.ds(lane0, 128)], tiles, load_sem.at[2])
    load_c = pltpu.make_async_copy(coef_ref, cbuf, load_sem.at[0])
    load_g = pltpu.make_async_copy(ints_ref, gbuf, load_sem.at[1])
    scalars = [
        pltpu.make_async_copy(pairs_hbm, pairs_ref, load_sem.at[4]),
        pltpu.make_async_copy(owner_hbm, owner_ref, load_sem.at[5]),
        pltpu.make_async_copy(slot_hbm, slot_ref, load_sem.at[6]),
    ]
    load_t.start()
    for copy in scalars:
        copy.start()
    load_c.start()
    load_g.start()

    def remote(src, dst, stage, device):
        return pltpu.make_async_remote_copy(
            src_ref=src,
            dst_ref=dst,
            send_sem=send_sem.at[stage],
            recv_sem=recv_sem.at[stage],
            device_id=device,
            device_id_type=MESH,
        )

    def all_of(part, stage):
        return remote(part, part, stage, (a, sib))

    za, zb, wa, wb, ids_at, pa, pb, fs, xs = range(9)
    ds = xs + mp

    load_t.wait()
    zbuf_a[own] = tiles[:, 0:8, :]
    zbuf_b[own] = tiles[:, 8:16, :]
    for copy in scalars:
        copy.wait()

    row_at = lax.broadcasted_iota(I32, (8, width), 0)
    lane_at = lax.broadcasted_iota(I32, (8, width), 1)
    note = jnp.zeros((8, width), I32)
    for chunk in range(chunks):
        for h in range(2):
            for u in range(8):
                if places[chunk][u][h] is not None:
                    s, t = places[chunk][u][h]
                    j = s * (lmb - 1) + t - (1 if t > s else 0)
                    place = slot_ref[j] * na + owner_ref[j] + 1
                    here = (row_at == 2 * chunk + h) & ((lane_at == a * 16 + u) | (lane_at == a * 16 + 8 + u))
                    note = jnp.where(here, place, note)
    for s in range(lmb):
        for k in range(2):
            here = (row_at == 2 * chunks) & (lane_at == a * 16 + 2 * s + k)
            note = jnp.where(here, pairs_ref[4 * s + 2 + k], note)
    msgs[a] = note

    pl.semaphore_wait(barrier, na + no - 2)

    def start_z(h, stage):
        for i in z_order:
            remote(zbuf[h].at[own], zbuf[h].at[own], stage, (a, ((z + i) % nz) * 2 + c)).start()

    start_z(0, za)

    def start_ids(i, _):
        remote(msgs.at[a], msgs.at[a], ids_at, (plane_peer(i), o)).start()
        return 0

    lax.fori_loop(0, na - 1, start_ids, 0)

    load_g.wait()
    height = bs * naux
    r_at = lax.broadcasted_iota(I32, (height, height), 0)
    c_at = lax.broadcasted_iota(I32, (height, height), 1)
    turn = (c_at == (r_at % bs) * naux + r_at // bs).astype(F32).astype(BF16)
    j = c_at - 2 * bs
    source = 2 * bs + (j // 8 % 2) * bs + (j // 16 % (bs // 16)) * 16 + (j // bs) * 8 + j % 8
    order = (r_at == jnp.where(c_at < 2 * bs, c_at, source)).astype(F32).astype(BF16)
    for s in range(lmb):
        block = gbuf[4 * s : 4 * s + 4].reshape(4 * bs, height)
        turned = lax.dot_general(turn, block, (((1,), (1,)), ((), ())), preferred_element_type=F32).astype(BF16)
        gt[s] = jnp.dot(turned, order, preferred_element_type=F32).astype(BF16)

    def swap(h, z_stage, w_stage):
        all_of(zbuf[h].at[pl.ds(0, (nz - 1) * per)], z_stage).wait_recv()
        for i in range(nz):
            part = zbuf[h].at[pl.ds((2 * i + c) * per, per)]
            remote(part, part, w_stage, (a, sib)).start()

    start_z(1, zb)

    load_c.wait()
    for s in range(lmb):
        for k in range(2):
            near[s, pl.ds(k * bs, bs), :] = cbuf[lax.rem(pairs_ref[4 * s + k], per)]
    xbuf[...] = jnp.zeros_like(xbuf)

    all_of(msgs.at[pl.ds(0, na - 1)], ids_at).wait_recv()
    ids = msgs[0]
    for src in range(1, na):
        ids = ids + msgs[src]
    asked[...] = ids[2 * chunks : 2 * chunks + 1, :]
    to_scalar = pltpu.make_async_copy(asked, idsm, load_sem.at[3])
    to_scalar.start()
    swap(0, za, wa)
    to_scalar.wait()

    def pair(h, to, s):
        return jnp.concatenate(
            [zbuf[h][idsm[0, to * 16 + 2 * s + k]] for k in range(2)], axis=0
        )

    def exchange(h, w_stage, p_stage):
        all_of(zbuf[h].at[pl.ds(0, nz * per)], w_stage).wait_recv()

        def pack(i, _):
            to = plane_peer(i)
            for s in range(lmb):
                packed[h, to, s] = pair(h, to, s)
            remote(packed.at[h, to], far.at[h, a], p_stage, (to, o)).start()
            return 0

        lax.fori_loop(0, na - 1, pack, 0)
        for s in range(lmb):
            far[h, a, s] = pair(h, a, s)

    exchange(0, wa, pa)
    swap(1, zb, wb)
    exchange(1, wb, pb)

    r_at = lax.broadcasted_iota(I32, (rows, width), 0) + 1
    l_at = (lax.broadcasted_iota(I32, (rows, width), 1) // 8) % 2
    for h in range(2):
        for tp in range(chunks):
            hit = r_at == ids[2 * tp + h : 2 * tp + h + 1, :]
            for m2 in range(2):
                onehot[pl.ds((m2 * 2 + h) * rows, rows), pl.ds(tp * width, width)] = (
                    jnp.where(hit & (l_at == m2), 1.0, 0.0).astype(BF16)
                )

    all_of(far.at[0, pl.ds(0, na - 1)], pa).wait_recv()
    all_of(far.at[1, pl.ds(0, na - 1)], pb).wait_recv()

    for s in range(lmb):
        there = [
            jnp.concatenate([far[h, g * nic + i, s] for h in range(2) for g in range(bs // 16)], axis=0)
            for i in range(nic)
        ]
        block = jnp.concatenate([near[s], jnp.concatenate(there, axis=1)], axis=0)
        halfway = jnp.dot(gt[s], block, preferred_element_type=F32).astype(BF16)
        for p in range(naux):
            hcat[pl.ds(s * bs, bs), pl.ds(p * nocc, nocc)] = halfway[p * bs : (p + 1) * bs]

    whole = hcat[...]
    products = lax.dot_general(whole, whole, (((1,), (1,)), ((), ())), preferred_element_type=F32)
    left = lax.broadcasted_iota(I32, (bs, 128), 1) < bs

    def block_half(place, h):
        s, t = place
        tile = products[s * bs : (s + 1) * bs, t // 2 * 128 : t // 2 * 128 + 128]
        return tile if t % 2 == h else pltpu.roll(tile, 64, 1)

    for chunk in range(chunks):
        for u in range(8):
            first, second = places[chunk][u]
            if first is not None:
                value = jnp.where(left, block_half(first, 0), block_half(second, 1))
                xbuf[chunk, pl.ds(u, bs, stride=8), :] = value

    def x_rows(e, q):
        at = pl.ds(pl.multiple_of((e * mp + q) * 16, 16), 16)
        return jnp.concatenate([xbuf[tp, at, :] for tp in range(chunks)], axis=1).astype(BF16)

    def send_x(q):
        def send(i, _):
            to = plane_peer(i)
            xsend[q, to] = x_rows(to, q)
            remote(xsend.at[q, to], xrecv.at[q, a], xs + q, (to, o)).start()
            return 0

        lax.fori_loop(0, na - 1, send, 0)

    for q in range(mp):
        send_x(q)
    for q in range(mp):
        xrecv[q, a] = x_rows(a, q)

    low = lax.broadcasted_iota(I32, (rows, 128), 1) < 64

    def send_d(q):
        all_of(xrecv.at[q, pl.ds(0, na - 1)], xs + q).wait_recv()
        right = [xrecv[q, :, :, pl.ds(tp * 128, 128)].reshape(width, 128) for tp in range(chunks)]
        right = jnp.concatenate(right, axis=0)
        z00, z01, z10, z11 = [
            jnp.dot(onehot[pl.ds(block * rows, rows), :], right, preferred_element_type=F32) for block in range(4)
        ]
        first = z00 + pltpu.roll(z01, 64, 1)
        second = pltpu.roll(z10, 64, 1) + z11
        dsend[q] = jnp.where(low, first, second).astype(BF16).reshape(no, na, 128)
        for i in o_order:
            to = (o + i) % no
            remote(dsend.at[q, to], drecv.at[q, o], ds + q, (a, to)).start()
        drecv[q, o] = dsend[q, o]

    for q in range(mp):
        send_d(q)
    for q in range(mp):
        all_of(drecv.at[q, pl.ds(0, no - 1)], ds + q).wait_recv()
        total = drecv[q, 0].astype(F32)
        for src in range(1, no):
            total = total + drecv[q, src].astype(F32)
        for r in range(na):
            fsend[r, :, pl.ds(q * 128, 128)] = total[r : r + 1, :]

    def send_f(i, _):
        to = plane_peer(i)
        remote(fsend.at[to], frecv.at[a], fs, (to, o)).start()
        return 0

    lax.fori_loop(0, na - 1, send_f, 0)
    frecv[a] = fsend[a]

    for h, (z_stage, w_stage, p_stage) in enumerate(((za, wa, pa), (zb, wb, pb))):
        all_of(zbuf[h].at[pl.ds(0, (nz - 1) * per)], z_stage).wait_send()
        all_of(zbuf[h].at[pl.ds(0, nz * per)], w_stage).wait_send()
        all_of(packed.at[h, pl.ds(0, na - 1)], p_stage).wait_send()
    all_of(msgs.at[pl.ds(0, na - 1)], ids_at).wait_send()
    for q in range(mp):
        all_of(xsend.at[q, pl.ds(0, na - 1)], xs + q).wait_send()
        all_of(dsend.at[q, pl.ds(0, no - 1)], ds + q).wait_send()
    all_of(frecv.at[pl.ds(0, na - 1)], fs).wait_recv()
    all_of(fsend.at[pl.ds(0, na - 1)], fs).wait_send()
    for e in range(na):
        out_ref[:, pl.ds(e * el, el)] = frecv[e]


def shards(integrals, coefficients, pair_list, partial_owner, partial_slot):
    na, no = lax.axis_size("aux"), lax.axis_size("orb")
    per, bs, nocc = coefficients.shape
    lmb = pair_list.shape[0] // 4
    naux = integrals.shape[2] // bs
    mp = bs // na // 2
    width = na * 16
    rows = na * no
    el = mp * 128
    chunks = (lmb - 2) // 2
    dims = (na, no, lmb, bs, nocc, naux, per)
    dma = pltpu.SemaphoreType.DMA
    vmem = pltpu.VMEM
    any_spec = pl.BlockSpec(memory_space=pltpu.HBM)
    return pl.pallas_call(
        functools.partial(kernel, dims),
        out_shape=jax.ShapeDtypeStruct((1, bs * bs), F32),
        in_specs=[any_spec] * 5,
        out_specs=pl.BlockSpec(memory_space=pltpu.VMEM),
        scratch_shapes=[
            pltpu.SMEM(pair_list.shape, I32),
            pltpu.SMEM(partial_slot.shape, I32),
            pltpu.SMEM(partial_slot.shape, I32),
            vmem(integrals.shape, BF16),
            vmem(coefficients.shape, BF16),
            vmem((per, 16, 128), BF16),
            vmem((no * per, 8, 128), BF16),
            vmem((no * per, 8, 128), BF16),
            vmem((na, 8, width), I32),
            vmem((1, width), I32),
            pltpu.SMEM((1, width), I32),
            vmem((2, na, lmb, 16, 128), BF16),
            vmem((lmb, 2 * bs, nocc), BF16),
            vmem((2, na, lmb, 16, 128), BF16),
            vmem((lmb, bs * naux, 4 * bs), BF16),
            vmem((lmb * bs, naux * nocc), BF16),
            vmem((chunks, bs * 8, 128), F32),
            vmem((mp, na, 16, chunks * 128), BF16),
            vmem((mp, na, 16, chunks * 128), BF16),
            vmem((4 * rows, chunks * width), BF16),
            vmem((mp, no, na, 128), BF16),
            vmem((mp, no, na, 128), BF16),
            vmem((na, 1, el), F32),
            vmem((na, 1, el), F32),
            dma((7,)),
            dma((8 + 2 * mp,)),
            dma((8 + 2 * mp,)),
        ],
        compiler_params=pltpu.CompilerParams(
            collective_id=0, has_side_effects=True, vmem_limit_bytes=60 * 2**20
        ),
    )(integrals, coefficients, pair_list, partial_owner.reshape(-1), partial_slot)


def solution(mesh):
    in_specs = (
        P(("aux", "orb"), None, None),
        P("orb", None, None),
        P(("aux", "orb")),
        P(("aux", "orb"), None),
        P(("aux", "orb")),
    )
    out_specs = P(("aux", "orb"), None)
    return jax.shard_map(shards, mesh=mesh, in_specs=in_specs, out_specs=out_specs, check_vma=False)
```

```python
import functools
import math

import jax
import jax.numpy as jnp
from jax import lax
from jax.experimental import pallas as pl
from jax.experimental.pallas import tpu as pltpu
from jax.sharding import PartitionSpec as P

MESH = pl.DeviceIdType.MESH
F32, BF16, I32 = jnp.float32, jnp.bfloat16, jnp.int32


def holders(side):
    def distance(at):
        return sum(abs(d) for d in at)

    offsets = range(-((side - 1) // 2), side // 2 + 1)
    plane = [(dx, dy) for dx in offsets for dy in offsets if 0 < distance((dx, dy)) and 2 * distance((dx, dy)) <= side + 1]
    reach = [(dx, dy) for dx in offsets for dy in offsets if 2 * (side - distance((dx, dy))) > side + 1]
    return plane, [(dx, dy, 1 if dx + dy >= 0 else -1) for dx, dy in reach]


def block_places(lmb):
    chunks = (lmb - 2) // 2
    places = [[[None, None] for _ in range(8)] for _ in range(chunks)]
    for chunk in range(chunks):
        for s in range(lmb):
            for h in range(2):
                places[chunk][s][h] = (s, (s + 2 * chunk + 1 + h) % lmb)
    for s in range(lmb):
        row, h = divmod(s, 2)
        places[row // 2][lmb + row % 2][h] = (s, (s + lmb - 1) % lmb)
    return places


def kernel(
    dims,
    ints_ref,
    coef_ref,
    pairs_hbm,
    owner_hbm,
    slot_hbm,
    out_ref,
    pairs_ref,
    owner_ref,
    slot_ref,
    gbuf,
    cbuf,
    tiles,
    zalt,
    zbuf_a,
    zbuf_b,
    msgs,
    crossmsgs,
    asked,
    idsm,
    packed,
    near,
    far,
    gt,
    hcat,
    xhalf,
    xbuf,
    xsend,
    xrecv,
    onehot,
    dsend,
    drecv,
    fsend,
    frecv,
    load_sem,
    send_sem,
    recv_sem,
):
    na, no, lmb, bs, nocc, naux, per = dims
    side = math.isqrt(na)
    nz = no // 2
    nic = nocc // 128
    mp = bs // na // 2
    chunks = (lmb - 2) // 2
    places = block_places(lmb)
    width = na * 16
    rows = na * no
    el = mp * 128
    a = lax.axis_index("aux")
    o = lax.axis_index("orb")
    x, y = a // side, a % side
    z, c = o // 2, o % 2
    sib = o + 1 - 2 * c
    piece = bs * nic // 2 // na
    groups = bs // piece
    near_by, crossed = holders(side)

    def plane_at(dx, dy):
        return ((x + dx) % side) * side + (y + dy) % side

    turned = (side // 2) * (z % 2)
    tile = plane_at(turned, turned)
    held = (tile, plane_at(side // 2 - turned, side // 2 - turned))
    own = pl.ds(o * per, per)
    zbuf = (zbuf_a, zbuf_b)

    def plane_peer(i):
        turn = na // 2 + side // 2
        j = jnp.where(i < na - turn, i + turn, i - (na - turn) + 1)
        return ((x + j // side) % side) * side + (y + j % side) % side

    z_order = sorted(range(1, nz), key=lambda i: -min(i, nz - i))
    o_order = sorted(range(1, no), key=lambda i: -min(i, no - i))

    barrier = pltpu.get_barrier_semaphore()
    for i in o_order:
        pl.semaphore_signal(barrier, inc=1, device_id=(a, (o + i) % no), device_id_type=MESH)

    def greet(i, _):
        pl.semaphore_signal(barrier, inc=1, device_id=(plane_peer(i), o), device_id_type=MESH)
        return 0

    lax.fori_loop(0, na - 1, greet, 0)
    extra = [at for at in crossed if at[:2] != (0, 0)]
    for dx, dy, dz in extra:
        there = (plane_at(dx, dy), ((z + dz) % nz) * 2 + c)
        pl.semaphore_signal(barrier, inc=1, device_id=there, device_id_type=MESH)

    load_t = [
        pltpu.make_async_copy(
            coef_ref.at[
                :,
                pl.ds(pl.multiple_of(held[v] % groups * piece // 16 * 16, 16), 16),
                pl.ds(pl.multiple_of((h * nic // 2 + held[v] // groups) * 128, 128), 128),
            ],
            tiles.at[v, h],
            load_sem.at[8 + 2 * v + h],
        )
        for v in range(2)
        for h in range(2)
    ]
    load_c = pltpu.make_async_copy(coef_ref, cbuf, load_sem.at[0])
    load_g = pltpu.make_async_copy(ints_ref, gbuf, load_sem.at[1])
    scalars = [
        pltpu.make_async_copy(pairs_hbm, pairs_ref, load_sem.at[4]),
        pltpu.make_async_copy(owner_hbm, owner_ref, load_sem.at[5]),
        pltpu.make_async_copy(slot_hbm, slot_ref, load_sem.at[6]),
    ]
    for copy in load_t:
        copy.start()
    for copy in scalars:
        copy.start()
    load_c.start()
    load_g.start()

    def remote(src, dst, stage, device):
        return pltpu.make_async_remote_copy(
            src_ref=src,
            dst_ref=dst,
            send_sem=send_sem.at[stage],
            recv_sem=recv_sem.at[stage],
            device_id=device,
            device_id_type=MESH,
        )

    def all_of(part, stage):
        return remote(part, part, stage, (a, sib))

    za, zb, wa, wb, ids_at, cross_at, pa, pb, fs, xs = range(10)
    ds = xs + mp

    for v in range(2):
        for h in range(2):
            load_t[2 * v + h].wait()
            part = tiles[v, h]
            if piece < 16:
                part = jnp.where(held[v] % groups % 2 == 0, part[:, :piece], part[:, piece:])
            if v == 0:
                zbuf[h][own] = part
            else:
                zalt[h] = part

    for copy in scalars:
        copy.wait()

    row_at = lax.broadcasted_iota(I32, (8, width), 0)
    lane_at = lax.broadcasted_iota(I32, (8, width), 1)
    note = jnp.zeros((8, width), I32)
    for chunk in range(chunks):
        for h in range(2):
            for u in range(8):
                if places[chunk][u][h] is not None:
                    s, t = places[chunk][u][h]
                    j = s * (lmb - 1) + t - (1 if t > s else 0)
                    place = slot_ref[j] * na + owner_ref[j] + 1
                    here = (row_at == 2 * chunk + h) & ((lane_at == a * 16 + u) | (lane_at == a * 16 + 8 + u))
                    note = jnp.where(here, place, note)
    for s in range(lmb):
        for k in range(2):
            here = (row_at == 2 * chunks) & (lane_at == a * 16 + 2 * s + k)
            note = jnp.where(here, pairs_ref[4 * s + 2 + k], note)
    msgs[a] = note

    pl.semaphore_wait(barrier, na + no - 2 + len(extra))

    def start_z(h, stage):
        for i in z_order:
            source = zbuf[h].at[own] if i % 2 == 0 else zalt.at[h]
            remote(source, zbuf[h].at[own], stage, (a, ((z + i) % nz) * 2 + c)).start()

    start_z(0, za)

    def start_ids(i, _):
        remote(msgs.at[a], msgs.at[a], ids_at, (plane_peer(i), o)).start()
        return 0

    for n, (dx, dy, dz) in enumerate(crossed):
        there = (plane_at(dx, dy), ((z + dz) % nz) * 2 + c)
        remote(msgs.at[a], crossmsgs.at[n], cross_at, there).start()
    lax.fori_loop(0, na - 1, start_ids, 0)

    load_g.wait()
    height = bs * naux
    r_at = lax.broadcasted_iota(I32, (height, height), 0)
    c_at = lax.broadcasted_iota(I32, (height, height), 1)
    turn = (c_at == (r_at % bs) * naux + r_at // bs).astype(F32).astype(BF16)
    j = c_at - 2 * bs
    source = 2 * bs + (j // piece % 2) * bs + (j // (2 * piece)) * piece + j % piece
    order = (r_at == jnp.where(c_at < 2 * bs, c_at, source)).astype(F32).astype(BF16)
    for s in range(lmb):
        block = gbuf[4 * s : 4 * s + 4].reshape(4 * bs, height)
        turned = lax.dot_general(turn, block, (((1,), (1,)), ((), ())), preferred_element_type=F32).astype(BF16)
        gt[s] = jnp.dot(turned, order, preferred_element_type=F32).astype(BF16)

    def swap(h, z_stage, w_stage):
        all_of(zbuf[h].at[pl.ds(0, (nz - 1) * per)], z_stage).wait_recv()
        for i in range(nz):
            part = zbuf[h].at[pl.ds((2 * i + c) * per, per)]
            remote(part, part, w_stage, (a, sib)).start()

    start_z(1, zb)

    load_c.wait()
    for s in range(lmb):
        for k in range(2):
            near[s, pl.ds(k * bs, bs), :] = cbuf[lax.rem(pairs_ref[4 * s + k], per)]
    xbuf[...] = jnp.zeros_like(xbuf)

    all_of(msgs.at[pl.ds(0, na - 1)], ids_at).wait_recv()
    ids = msgs[0]
    for src in range(1, na):
        ids = ids + msgs[src]
    asked[0:1, :] = ids[2 * chunks : 2 * chunks + 1, :]
    all_of(crossmsgs, cross_at).wait_recv()
    others = crossmsgs[0]
    for n in range(1, len(crossed)):
        others = others + crossmsgs[n]
    asked[1:2, :] = others[2 * chunks : 2 * chunks + 1, :]
    to_scalar = pltpu.make_async_copy(asked, idsm, load_sem.at[3])
    to_scalar.start()
    swap(0, za, wa)
    to_scalar.wait()

    def pair(h, row, asker, s):
        return jnp.concatenate([zbuf[h][idsm[row, asker * 16 + 2 * s + k]] for k in range(2)], axis=0)

    def exchange(h, w_stage, p_stage):
        all_of(zbuf[h].at[pl.ds(0, nz * per)], w_stage).wait_recv()
        served = [(0, plane_at(dx, dy), o) for dx, dy in near_by if abs(dx) + abs(dy) > 1]
        served += [(1, plane_at(-dx, -dy), ((z - dz) % nz) * 2 + c) for dx, dy, dz in crossed]
        served += [(0, plane_at(dx, dy), o) for dx, dy in near_by if abs(dx) + abs(dy) == 1]
        for n, (row, asker, orb) in enumerate(served):
            for s in range(lmb):
                packed[h, n, s] = pair(h, row, asker, s)
            remote(packed.at[h, n], far.at[h, tile], p_stage, (asker, orb)).start()
        for s in range(lmb):
            far[h, tile, s] = pair(h, 0, a, s)

    exchange(0, wa, pa)
    swap(1, zb, wb)
    exchange(1, wb, pb)

    r_at = lax.broadcasted_iota(I32, (rows, width), 0) + 1
    l_at = (lax.broadcasted_iota(I32, (rows, width), 1) // 8) % 2
    for h in range(2):
        for tp in range(chunks):
            hit = r_at == ids[2 * tp + h : 2 * tp + h + 1, :]
            for m2 in range(2):
                onehot[pl.ds((m2 * 2 + h) * rows, rows), pl.ds(tp * width, width)] = (
                    jnp.where(hit & (l_at == m2), 1.0, 0.0).astype(BF16)
                )

    def multiply(h, p_stage):
        all_of(far.at[h, pl.ds(0, na - 1)], p_stage).wait_recv()
        wide = nocc // 2
        for s in range(lmb):
            there = [
                jnp.concatenate([far[h, i * groups + g, s] for g in range(groups)], axis=0) for i in range(nic // 2)
            ]
            there = jnp.concatenate(there, axis=1) if nic > 2 else there[0]
            block = jnp.concatenate([near[s, :, pl.ds(h * wide, wide)], there], axis=0)
            halfway = jnp.dot(gt[s], block, preferred_element_type=F32).astype(BF16)
            for p in range(naux):
                hcat[h, pl.ds(s * bs, bs), pl.ds(p * wide, wide)] = halfway[p * bs : (p + 1) * bs]
        whole = hcat[h]
        return lax.dot_general(whole, whole, (((1,), (1,)), ((), ())), preferred_element_type=F32)

    xhalf[...] = multiply(0, pa)
    products = xhalf[...] + multiply(1, pb)
    left = lax.broadcasted_iota(I32, (bs, 128), 1) < bs

    def block_half(place, h):
        s, t = place
        tile = products[s * bs : (s + 1) * bs, t // 2 * 128 : t // 2 * 128 + 128]
        return tile if t % 2 == h else pltpu.roll(tile, 64, 1)

    for chunk in range(chunks):
        for u in range(8):
            first, second = places[chunk][u]
            if first is not None:
                value = jnp.where(left, block_half(first, 0), block_half(second, 1))
                xbuf[chunk, pl.ds(u, bs, stride=8), :] = value

    def x_rows(e, q):
        at = pl.ds(pl.multiple_of((e * mp + q) * 16, 16), 16)
        return jnp.concatenate([xbuf[tp, at, :] for tp in range(chunks)], axis=1).astype(BF16)

    def send_x(q):
        def send(i, _):
            to = plane_peer(i)
            xsend[q, to] = x_rows(to, q)
            remote(xsend.at[q, to], xrecv.at[q, a], xs + q, (to, o)).start()
            return 0

        lax.fori_loop(0, na - 1, send, 0)

    for q in range(mp):
        send_x(q)
    for q in range(mp):
        xrecv[q, a] = x_rows(a, q)

    low = lax.broadcasted_iota(I32, (rows, 128), 1) < 64

    def send_d(q):
        all_of(xrecv.at[q, pl.ds(0, na - 1)], xs + q).wait_recv()
        right = [xrecv[q, :, :, pl.ds(tp * 128, 128)].reshape(width, 128) for tp in range(chunks)]
        right = jnp.concatenate(right, axis=0)
        z00, z01, z10, z11 = [
            jnp.dot(onehot[pl.ds(block * rows, rows), :], right, preferred_element_type=F32) for block in range(4)
        ]
        first = z00 + pltpu.roll(z01, 64, 1)
        second = pltpu.roll(z10, 64, 1) + z11
        dsend[q] = jnp.where(low, first, second).astype(BF16).reshape(no, na, 128)
        for i in o_order:
            to = (o + i) % no
            remote(dsend.at[q, to], drecv.at[q, o], ds + q, (a, to)).start()
        drecv[q, o] = dsend[q, o]

    for q in range(mp):
        send_d(q)
    for q in range(mp):
        all_of(drecv.at[q, pl.ds(0, no - 1)], ds + q).wait_recv()
        total = drecv[q, 0].astype(F32)
        for src in range(1, no):
            total = total + drecv[q, src].astype(F32)
        for r in range(na):
            fsend[r, :, pl.ds(q * 128, 128)] = total[r : r + 1, :]

    def send_f(i, _):
        to = plane_peer(i)
        remote(fsend.at[to], frecv.at[a], fs, (to, o)).start()
        return 0

    lax.fori_loop(0, na - 1, send_f, 0)
    frecv[a] = fsend[a]

    for h, (z_stage, w_stage, p_stage) in enumerate(((za, wa, pa), (zb, wb, pb))):
        all_of(zbuf[h].at[pl.ds(0, (nz - 1) * per)], z_stage).wait_send()
        all_of(zbuf[h].at[pl.ds(0, nz * per)], w_stage).wait_send()
        all_of(packed.at[h, pl.ds(0, na - 1)], p_stage).wait_send()
    all_of(msgs.at[pl.ds(0, na - 1)], ids_at).wait_send()
    all_of(crossmsgs, cross_at).wait_send()
    for q in range(mp):
        all_of(xsend.at[q, pl.ds(0, na - 1)], xs + q).wait_send()
        all_of(dsend.at[q, pl.ds(0, no - 1)], ds + q).wait_send()
    all_of(frecv.at[pl.ds(0, na - 1)], fs).wait_recv()
    all_of(fsend.at[pl.ds(0, na - 1)], fs).wait_send()
    for e in range(na):
        out_ref[:, pl.ds(e * el, el)] = frecv[e]


def shards(integrals, coefficients, pair_list, partial_owner, partial_slot):
    na, no = lax.axis_size("aux"), lax.axis_size("orb")
    per, bs, nocc = coefficients.shape
    lmb = pair_list.shape[0] // 4
    naux = integrals.shape[2] // bs
    mp = bs // na // 2
    width = na * 16
    rows = na * no
    el = mp * 128
    chunks = (lmb - 2) // 2
    piece = bs * nocc // 256 // na
    dims = (na, no, lmb, bs, nocc, naux, per)
    dma = pltpu.SemaphoreType.DMA
    vmem = pltpu.VMEM
    any_spec = pl.BlockSpec(memory_space=pltpu.HBM)
    return pl.pallas_call(
        functools.partial(kernel, dims),
        out_shape=jax.ShapeDtypeStruct((1, bs * bs), F32),
        in_specs=[any_spec] * 5,
        out_specs=pl.BlockSpec(memory_space=pltpu.VMEM),
        scratch_shapes=[
            pltpu.SMEM(pair_list.shape, I32),
            pltpu.SMEM(partial_slot.shape, I32),
            pltpu.SMEM(partial_slot.shape, I32),
            vmem(integrals.shape, BF16),
            vmem(coefficients.shape, BF16),
            vmem((2, 2, per, 16, 128), BF16),
            vmem((2, per, piece, 128), BF16),
            vmem((no * per, piece, 128), BF16),
            vmem((no * per, piece, 128), BF16),
            vmem((na, 8, width), I32),
            vmem((len(holders(math.isqrt(na))[1]), 8, width), I32),
            vmem((2, width), I32),
            pltpu.SMEM((2, width), I32),
            vmem((2, na, lmb, 2 * piece, 128), BF16),
            vmem((lmb, 2 * bs, nocc), BF16),
            vmem((2, na, lmb, 2 * piece, 128), BF16),
            vmem((lmb, bs * naux, 4 * bs), BF16),
            vmem((2, lmb * bs, naux * nocc // 2), BF16),
            vmem((lmb * bs, lmb * bs), F32),
            vmem((chunks, bs * 8, 128), F32),
            vmem((mp, na, 16, chunks * 128), BF16),
            vmem((mp, na, 16, chunks * 128), BF16),
            vmem((4 * rows, chunks * width), BF16),
            vmem((mp, no, na, 128), BF16),
            vmem((mp, no, na, 128), BF16),
            vmem((na, 1, el), F32),
            vmem((na, 1, el), F32),
            dma((12,)),
            dma((9 + 2 * mp,)),
            dma((9 + 2 * mp,)),
        ],
        compiler_params=pltpu.CompilerParams(
            collective_id=0, has_side_effects=True, vmem_limit_bytes=56098816
        ),
    )(integrals, coefficients, pair_list, partial_owner.reshape(-1), partial_slot)


def solution(mesh):
    in_specs = (
        P(("aux", "orb"), None, None),
        P("orb", None, None),
        P(("aux", "orb")),
        P(("aux", "orb"), None),
        P(("aux", "orb")),
    )
    out_specs = P(("aux", "orb"), None)
    return jax.shard_map(shards, mesh=mesh, in_specs=in_specs, out_specs=out_specs, check_vma=False)
```

```python
import functools
import math

import jax
import jax.numpy as jnp
from jax import lax
from jax.experimental import pallas as pl
from jax.experimental.pallas import tpu as pltpu
from jax.sharding import PartitionSpec as P

MESH = pl.DeviceIdType.MESH
F32, BF16, I32 = jnp.float32, jnp.bfloat16, jnp.int32


def holders(side):
    def distance(at):
        return sum(abs(d) for d in at)

    offsets = range(-((side - 1) // 2), side // 2 + 1)
    plane = [(dx, dy) for dx in offsets for dy in offsets if 0 < distance((dx, dy)) and 2 * distance((dx, dy)) <= side + 1]
    reach = [(dx, dy) for dx in offsets for dy in offsets if 2 * (side - distance((dx, dy))) > side + 1]
    return plane, [(dx, dy, 1 if dx + dy >= 0 else -1) for dx, dy in reach]


def block_places(lmb):
    chunks = (lmb - 2) // 2
    places = [[[None, None] for _ in range(8)] for _ in range(chunks)]
    for chunk in range(chunks):
        for s in range(lmb):
            for h in range(2):
                places[chunk][s][h] = (s, (s + 2 * chunk + 1 + h) % lmb)
    for s in range(lmb):
        row, h = divmod(s, 2)
        places[row // 2][lmb + row % 2][h] = (s, (s + lmb - 1) % lmb)
    return places


def kernel(
    dims,
    ints_ref,
    coef_ref,
    pairs_hbm,
    owner_hbm,
    slot_hbm,
    out_ref,
    pairs_ref,
    owner_ref,
    slot_ref,
    gbuf,
    cbuf,
    tiles,
    zalt,
    zbuf_a,
    zbuf_b,
    msgs,
    crossnote,
    asked,
    idsm,
    packed,
    near,
    far,
    gt,
    hcat,
    xhalf,
    xbuf,
    xsend,
    xrecv,
    onehot,
    dsend,
    drecv,
    fsend,
    frecv,
    load_sem,
    send_sem,
    recv_sem,
):
    na, no, lmb, bs, nocc, naux, per = dims
    side = math.isqrt(na)
    nz = no // 2
    nic = nocc // 128
    mp = bs // na // 2
    chunks = (lmb - 2) // 2
    places = block_places(lmb)
    width = na * 16
    rows = na * no
    el = mp * 128
    a = lax.axis_index("aux")
    o = lax.axis_index("orb")
    x, y = a // side, a % side
    z, c = o // 2, o % 2
    sib = o + 1 - 2 * c
    piece = bs * nic // 2 // na
    groups = bs // piece
    near_by, crossed = holders(side)

    def plane_at(dx, dy):
        return ((x + dx) % side) * side + (y + dy) % side

    turned = (side // 2) * (z % 2)
    tile = plane_at(turned, turned)
    shift = side // 2
    held = (tile, plane_at(shift - turned, shift - turned))
    opposite = plane_at(shift, shift)
    served_by = [(plane_at(dx, dy), o, plane_at(dx + turned, dy + turned), a) for dx, dy in near_by if abs(dx) + abs(dy) > 1]
    served_by += [
        (plane_at(dx, dy), ((z + dz) % nz) * 2 + c, plane_at(dx + shift - turned, dy + shift - turned), opposite)
        for dx, dy, dz in crossed
    ]
    served_by += [(plane_at(dx, dy), o, plane_at(dx + turned, dy + turned), a) for dx, dy in near_by if abs(dx) + abs(dy) == 1]
    own = pl.ds(o * per, per)
    zbuf = (zbuf_a, zbuf_b)

    def plane_peer(i):
        turn = na // 2 + side // 2
        j = jnp.where(i < na - turn, i + turn, i - (na - turn) + 1)
        return ((x + j // side) % side) * side + (y + j % side) % side

    z_order = sorted(range(1, nz), key=lambda i: -min(i, nz - i))
    o_order = sorted(range(1, no), key=lambda i: -min(i, no - i))

    barrier = pltpu.get_barrier_semaphore()
    for i in o_order:
        pl.semaphore_signal(barrier, inc=1, device_id=(a, (o + i) % no), device_id_type=MESH)

    def greet(i, _):
        pl.semaphore_signal(barrier, inc=1, device_id=(plane_peer(i), o), device_id_type=MESH)
        return 0

    lax.fori_loop(0, na - 1, greet, 0)
    extra = [at for at in crossed if at[:2] != (0, 0)]
    for dx, dy, dz in extra:
        there = (plane_at(dx, dy), ((z + dz) % nz) * 2 + c)
        pl.semaphore_signal(barrier, inc=1, device_id=there, device_id_type=MESH)

    load_t = [
        pltpu.make_async_copy(
            coef_ref.at[
                :,
                pl.ds(pl.multiple_of(held[v] % groups * piece // 16 * 16, 16), 16),
                pl.ds(pl.multiple_of((h * nic // 2 + held[v] // groups) * 128, 128), 128),
            ],
            tiles.at[v, h],
            load_sem.at[8 + 2 * v + h],
        )
        for v in range(2)
        for h in range(2)
    ]
    load_c = pltpu.make_async_copy(coef_ref, cbuf, load_sem.at[0])
    load_g = pltpu.make_async_copy(ints_ref, gbuf, load_sem.at[1])
    scalars = [
        pltpu.make_async_copy(pairs_hbm, pairs_ref, load_sem.at[4]),
        pltpu.make_async_copy(owner_hbm, owner_ref, load_sem.at[5]),
        pltpu.make_async_copy(slot_hbm, slot_ref, load_sem.at[6]),
    ]
    for copy in load_t:
        copy.start()
    for copy in scalars:
        copy.start()
    load_c.start()
    load_g.start()

    def remote(src, dst, stage, device):
        return pltpu.make_async_remote_copy(
            src_ref=src,
            dst_ref=dst,
            send_sem=send_sem.at[stage],
            recv_sem=recv_sem.at[stage],
            device_id=device,
            device_id_type=MESH,
        )

    def all_of(part, stage):
        return remote(part, part, stage, (a, sib))

    za, zb, wa, wb, ids_at, pa, pb, fs, xs = range(9)
    ds = xs + mp

    for v in range(2):
        for h in range(2):
            load_t[2 * v + h].wait()
            part = tiles[v, h]
            if piece < 16:
                part = jnp.where(held[v] % groups % 2 == 0, part[:, :piece], part[:, piece:])
            if v == 0:
                zbuf[h][own] = part
            else:
                zalt[h] = part

    for copy in scalars:
        copy.wait()

    row_at = lax.broadcasted_iota(I32, (8, width), 0)
    lane_at = lax.broadcasted_iota(I32, (8, width), 1)
    note = jnp.zeros((8, width), I32)
    for chunk in range(chunks):
        for h in range(2):
            for u in range(8):
                if places[chunk][u][h] is not None:
                    s, t = places[chunk][u][h]
                    j = s * (lmb - 1) + t - (1 if t > s else 0)
                    place = slot_ref[j] * na + owner_ref[j] + 1
                    here = (row_at == 2 * chunk + h) & ((lane_at == a * 16 + u) | (lane_at == a * 16 + 8 + u))
                    note = jnp.where(here, place, note)
    for s in range(lmb):
        for k in range(2):
            here = (row_at == 2 * chunks) & (lane_at == a * 16 + 2 * s + k)
            note = jnp.where(here, pairs_ref[4 * s + 2 + k], note)
    msgs[a] = note
    crossnote[...] = pltpu.roll(note, lax.rem(opposite + na - a, na) * 16, 1)

    pl.semaphore_wait(barrier, na + no - 2 + len(extra))

    def start_z(h, stage):
        for i in z_order:
            source = zbuf[h].at[own] if i % 2 == 0 else zalt.at[h]
            remote(source, zbuf[h].at[own], stage, (a, ((z + i) % nz) * 2 + c)).start()

    start_z(0, za)

    for there, orb, _, number in served_by:
        source = crossnote if number is opposite else msgs.at[a]
        remote(source, msgs.at[number], ids_at, (there, orb)).start()

    load_g.wait()
    height = bs * naux
    r_at = lax.broadcasted_iota(I32, (height, height), 0)
    c_at = lax.broadcasted_iota(I32, (height, height), 1)
    turn = (c_at == (r_at % bs) * naux + r_at // bs).astype(F32).astype(BF16)
    j = c_at - 2 * bs
    source = 2 * bs + (j // piece % 2) * bs + (j // (2 * piece)) * piece + j % piece
    order = (r_at == jnp.where(c_at < 2 * bs, c_at, source)).astype(F32).astype(BF16)
    for s in range(lmb):
        block = gbuf[4 * s : 4 * s + 4].reshape(4 * bs, height)
        turned = lax.dot_general(turn, block, (((1,), (1,)), ((), ())), preferred_element_type=F32).astype(BF16)
        gt[s] = jnp.dot(turned, order, preferred_element_type=F32).astype(BF16)

    def swap(h, z_stage, w_stage):
        all_of(zbuf[h].at[pl.ds(0, (nz - 1) * per)], z_stage).wait_recv()
        for i in range(nz):
            part = zbuf[h].at[pl.ds((2 * i + c) * per, per)]
            remote(part, part, w_stage, (a, sib)).start()

    start_z(1, zb)

    load_c.wait()
    for s in range(lmb):
        for k in range(2):
            near[s, pl.ds(k * bs, bs), :] = cbuf[lax.rem(pairs_ref[4 * s + k], per)]
    xbuf[...] = jnp.zeros_like(xbuf)

    all_of(msgs.at[pl.ds(0, na - 1)], ids_at).wait_recv()
    ids = msgs[0]
    for src in range(1, na):
        ids = ids + msgs[src]
    asked[...] = ids[2 * chunks : 2 * chunks + 1, :]
    to_scalar = pltpu.make_async_copy(asked, idsm, load_sem.at[3])
    to_scalar.start()
    swap(0, za, wa)
    to_scalar.wait()

    def pair(h, number, s):
        return jnp.concatenate([zbuf[h][idsm[0, number * 16 + 2 * s + k]] for k in range(2)], axis=0)

    def exchange(h, w_stage, p_stage):
        all_of(zbuf[h].at[pl.ds(0, nz * per)], w_stage).wait_recv()
        served = [(plane_at(dx, dy), plane_at(dx, dy), o) for dx, dy in near_by if abs(dx) + abs(dy) > 1]
        served += [
            (plane_at(shift - dx, shift - dy), plane_at(-dx, -dy), ((z - dz) % nz) * 2 + c) for dx, dy, dz in crossed
        ]
        served += [(plane_at(dx, dy), plane_at(dx, dy), o) for dx, dy in near_by if abs(dx) + abs(dy) == 1]
        for n, (number, asker, orb) in enumerate(served):
            for s in range(lmb):
                packed[h, n, s] = pair(h, number, s)
            remote(packed.at[h, n], far.at[h, tile], p_stage, (asker, orb)).start()
        for s in range(lmb):
            far[h, tile, s] = pair(h, a, s)

    exchange(0, wa, pa)
    swap(1, zb, wb)
    exchange(1, wb, pb)

    r_at = lax.broadcasted_iota(I32, (rows, width), 0) + 1
    l_at = (lax.broadcasted_iota(I32, (rows, width), 1) // 8) % 2
    for h in range(2):
        for tp in range(chunks):
            hit = r_at == ids[2 * tp + h : 2 * tp + h + 1, :]
            for m2 in range(2):
                onehot[pl.ds((m2 * 2 + h) * rows, rows), pl.ds(tp * width, width)] = (
                    jnp.where(hit & (l_at == m2), 1.0, 0.0).astype(BF16)
                )

    def multiply(h, p_stage):
        all_of(far.at[h, pl.ds(0, na - 1)], p_stage).wait_recv()
        wide = nocc // 2
        for s in range(lmb):
            there = [
                jnp.concatenate([far[h, i * groups + g, s] for g in range(groups)], axis=0) for i in range(nic // 2)
            ]
            there = jnp.concatenate(there, axis=1) if nic > 2 else there[0]
            block = jnp.concatenate([near[s, :, pl.ds(h * wide, wide)], there], axis=0)
            halfway = jnp.dot(gt[s], block, preferred_element_type=F32).astype(BF16)
            for p in range(naux):
                hcat[h, pl.ds(s * bs, bs), pl.ds(p * wide, wide)] = halfway[p * bs : (p + 1) * bs]
        whole = hcat[h]
        return lax.dot_general(whole, whole, (((1,), (1,)), ((), ())), preferred_element_type=F32)

    xhalf[...] = multiply(0, pa)
    products = xhalf[...] + multiply(1, pb)
    left = lax.broadcasted_iota(I32, (bs, 128), 1) < bs

    def block_half(place, h):
        s, t = place
        tile = products[s * bs : (s + 1) * bs, t // 2 * 128 : t // 2 * 128 + 128]
        return tile if t % 2 == h else pltpu.roll(tile, 64, 1)

    for chunk in range(chunks):
        for u in range(8):
            first, second = places[chunk][u]
            if first is not None:
                value = jnp.where(left, block_half(first, 0), block_half(second, 1))
                xbuf[chunk, pl.ds(u, bs, stride=8), :] = value

    def x_rows(e, q):
        at = pl.ds(pl.multiple_of((e * mp + q) * 16, 16), 16)
        return jnp.concatenate([xbuf[tp, at, :] for tp in range(chunks)], axis=1).astype(BF16)

    for q in range(mp):
        for n, (there, orb, e, number) in enumerate(served_by):
            xsend[q, n] = x_rows(e, q)
            remote(xsend.at[q, n], xrecv.at[q, number], xs + q, (there, orb)).start()
    for q in range(mp):
        xrecv[q, a] = x_rows(tile, q)

    low = lax.broadcasted_iota(I32, (rows, 128), 1) < 64

    def send_d(q):
        all_of(xrecv.at[q, pl.ds(0, na - 1)], xs + q).wait_recv()
        right = [xrecv[q, :, :, pl.ds(tp * 128, 128)].reshape(width, 128) for tp in range(chunks)]
        right = jnp.concatenate(right, axis=0)
        z00, z01, z10, z11 = [
            jnp.dot(onehot[pl.ds(block * rows, rows), :], right, preferred_element_type=F32) for block in range(4)
        ]
        first = z00 + pltpu.roll(z01, 64, 1)
        second = pltpu.roll(z10, 64, 1) + z11
        dsend[q] = jnp.where(low, first, second).astype(BF16).reshape(no, na, 128)
        for i in o_order:
            to = (o + i) % no
            remote(dsend.at[q, to], drecv.at[q, o], ds + q, (a, to)).start()
        drecv[q, o] = dsend[q, o]

    for q in range(mp):
        send_d(q)
    for q in range(mp):
        all_of(drecv.at[q, pl.ds(0, no - 1)], ds + q).wait_recv()
        for v in range(2):
            total = None
            for src in range(no):
                if src // 2 % 2 == v:
                    term = drecv[q, src].astype(F32)
                    total = term if total is None else total + term
            for r in range(na):
                fsend[r, :, pl.ds(v * el + q * 128, 128)] = total[r : r + 1, :]

    def send_f(i, _):
        to = plane_peer(i)
        remote(fsend.at[to], frecv.at[a], fs, (to, o)).start()
        return 0

    lax.fori_loop(0, na - 1, send_f, 0)
    frecv[a] = fsend[a]

    for h, (z_stage, w_stage, p_stage) in enumerate(((za, wa, pa), (zb, wb, pb))):
        all_of(zbuf[h].at[pl.ds(0, (nz - 1) * per)], z_stage).wait_send()
        all_of(zbuf[h].at[pl.ds(0, nz * per)], w_stage).wait_send()
        all_of(packed.at[h, pl.ds(0, na - 1)], p_stage).wait_send()
    all_of(msgs.at[pl.ds(0, na - 1)], ids_at).wait_send()
    for q in range(mp):
        all_of(xsend.at[q, pl.ds(0, na - 1)], xs + q).wait_send()
        all_of(dsend.at[q, pl.ds(0, no - 1)], ds + q).wait_send()
    all_of(frecv.at[pl.ds(0, na - 1)], fs).wait_recv()
    all_of(fsend.at[pl.ds(0, na - 1)], fs).wait_send()
    for e in range(na):
        other = (e // side + side // 2) % side * side + (e % side + side // 2) % side
        out_ref[:, pl.ds(e * el, el)] = frecv[e, :, pl.ds(0, el)] + frecv[other, :, pl.ds(el, el)]


def shards(integrals, coefficients, pair_list, partial_owner, partial_slot):
    na, no = lax.axis_size("aux"), lax.axis_size("orb")
    per, bs, nocc = coefficients.shape
    lmb = pair_list.shape[0] // 4
    naux = integrals.shape[2] // bs
    mp = bs // na // 2
    width = na * 16
    rows = na * no
    el = mp * 128
    chunks = (lmb - 2) // 2
    piece = bs * nocc // 256 // na
    dims = (na, no, lmb, bs, nocc, naux, per)
    dma = pltpu.SemaphoreType.DMA
    vmem = pltpu.VMEM
    any_spec = pl.BlockSpec(memory_space=pltpu.HBM)
    return pl.pallas_call(
        functools.partial(kernel, dims),
        out_shape=jax.ShapeDtypeStruct((1, bs * bs), F32),
        in_specs=[any_spec] * 5,
        out_specs=pl.BlockSpec(memory_space=pltpu.VMEM),
        scratch_shapes=[
            pltpu.SMEM(pair_list.shape, I32),
            pltpu.SMEM(partial_slot.shape, I32),
            pltpu.SMEM(partial_slot.shape, I32),
            vmem(integrals.shape, BF16),
            vmem(coefficients.shape, BF16),
            vmem((2, 2, per, 16, 128), BF16),
            vmem((2, per, piece, 128), BF16),
            vmem((no * per, piece, 128), BF16),
            vmem((no * per, piece, 128), BF16),
            vmem((na, 8, width), I32),
            vmem((8, width), I32),
            vmem((1, width), I32),
            pltpu.SMEM((1, width), I32),
            vmem((2, na, lmb, 2 * piece, 128), BF16),
            vmem((lmb, 2 * bs, nocc), BF16),
            vmem((2, na, lmb, 2 * piece, 128), BF16),
            vmem((lmb, bs * naux, 4 * bs), BF16),
            vmem((2, lmb * bs, naux * nocc // 2), BF16),
            vmem((lmb * bs, lmb * bs), F32),
            vmem((chunks, bs * 8, 128), F32),
            vmem((mp, na, 16, chunks * 128), BF16),
            vmem((mp, na, 16, chunks * 128), BF16),
            vmem((4 * rows, chunks * width), BF16),
            vmem((mp, no, na, 128), BF16),
            vmem((mp, no, na, 128), BF16),
            vmem((na, 1, 2 * el), F32),
            vmem((na, 1, 2 * el), F32),
            dma((12,)),
            dma((8 + 2 * mp,)),
            dma((8 + 2 * mp,)),
        ],
        compiler_params=pltpu.CompilerParams(
            collective_id=0, has_side_effects=True, vmem_limit_bytes=56098816
        ),
    )(integrals, coefficients, pair_list, partial_owner.reshape(-1), partial_slot)


def solution(mesh):
    in_specs = (
        P(("aux", "orb"), None, None),
        P("orb", None, None),
        P(("aux", "orb")),
        P(("aux", "orb"), None),
        P(("aux", "orb")),
    )
    out_specs = P(("aux", "orb"), None)
    return jax.shard_map(shards, mesh=mesh, in_specs=in_specs, out_specs=out_specs, check_vma=False)
```

```python
import functools
import math

import jax
import jax.numpy as jnp
from jax import lax
from jax.experimental import pallas as pl
from jax.experimental.pallas import tpu as pltpu
from jax.sharding import PartitionSpec as P

MESH = pl.DeviceIdType.MESH
F32, BF16, I32 = jnp.float32, jnp.bfloat16, jnp.int32


def holders(side):
    def distance(at):
        return sum(abs(d) for d in at)

    offsets = range(-((side - 1) // 2), side // 2 + 1)
    plane = [(dx, dy) for dx in offsets for dy in offsets if 0 < distance((dx, dy)) and 2 * distance((dx, dy)) <= side + 1]
    reach = [(dx, dy) for dx in offsets for dy in offsets if 2 * (side - distance((dx, dy))) > side + 1]
    return plane, [(dx, dy, 1 if dx + dy >= 0 else -1) for dx, dy in reach]


def block_places(lmb):
    chunks = (lmb - 2) // 2
    places = [[[None, None] for _ in range(8)] for _ in range(chunks)]
    for chunk in range(chunks):
        for s in range(lmb):
            for h in range(2):
                places[chunk][s][h] = (s, (s + 2 * chunk + 1 + h) % lmb)
    for s in range(lmb):
        row, h = divmod(s, 2)
        places[row // 2][lmb + row % 2][h] = (s, (s + lmb - 1) % lmb)
    return places


def kernel(
    dims,
    ints_ref,
    coef_ref,
    pairs_hbm,
    owner_hbm,
    slot_hbm,
    out_ref,
    pairs_ref,
    owner_ref,
    slot_ref,
    gbuf,
    cbuf,
    tiles,
    zalt,
    zbuf_a,
    zbuf_b,
    msgs,
    crossnote,
    asked,
    idsm,
    packed,
    near,
    far,
    gt,
    hcat,
    xhalf,
    xbuf,
    xsend,
    xrecv,
    onehot,
    dsend,
    drecv,
    fsend,
    frecv,
    load_sem,
    send_sem,
    recv_sem,
):
    na, no, lmb, bs, nocc, naux, per = dims
    side = math.isqrt(na)
    nz = no // 2
    nic = nocc // 128
    mp = bs // na // 2
    chunks = (lmb - 2) // 2
    places = block_places(lmb)
    width = na * 16
    rows = na * no
    el = mp * 128
    a = lax.axis_index("aux")
    o = lax.axis_index("orb")
    x, y = a // side, a % side
    z, c = o // 2, o % 2
    sib = o + 1 - 2 * c
    piece = bs * nic // 2 // na
    groups = bs // piece
    near_by, crossed = holders(side)

    def plane_at(dx, dy):
        return ((x + dx) % side) * side + (y + dy) % side

    turned = (side // 2) * (z % 2)
    tile = plane_at(turned, turned)
    shift = side // 2
    held = (tile, plane_at(shift - turned, shift - turned))
    opposite = plane_at(shift, shift)
    served_by = [(plane_at(dx, dy), o, plane_at(dx + turned, dy + turned), a) for dx, dy in near_by if abs(dx) + abs(dy) > 1]
    served_by += [
        (plane_at(dx, dy), ((z + dz) % nz) * 2 + c, plane_at(dx + shift - turned, dy + shift - turned), opposite)
        for dx, dy, dz in crossed
    ]
    served_by += [(plane_at(dx, dy), o, plane_at(dx + turned, dy + turned), a) for dx, dy in near_by if abs(dx) + abs(dy) == 1]
    own = pl.ds(o * per, per)
    zbuf = (zbuf_a, zbuf_b)

    def plane_peer(i):
        turn = na // 2 + side // 2
        j = jnp.where(i < na - turn, i + turn, i - (na - turn) + 1)
        return ((x + j // side) % side) * side + (y + j % side) % side

    z_order = sorted(range(1, nz), key=lambda i: -min(i, nz - i))
    o_order = sorted(range(1, no), key=lambda i: -min(i, no - i))

    barrier = pltpu.get_barrier_semaphore()
    for i in o_order:
        pl.semaphore_signal(barrier, inc=1, device_id=(a, (o + i) % no), device_id_type=MESH)

    def greet(i, _):
        pl.semaphore_signal(barrier, inc=1, device_id=(plane_peer(i), o), device_id_type=MESH)
        return 0

    lax.fori_loop(0, na - 1, greet, 0)
    extra = [at for at in crossed if at[:2] != (0, 0)]
    for dx, dy, dz in extra:
        there = (plane_at(dx, dy), ((z + dz) % nz) * 2 + c)
        pl.semaphore_signal(barrier, inc=1, device_id=there, device_id_type=MESH)

    load_t = [
        pltpu.make_async_copy(
            coef_ref.at[
                :,
                pl.ds(pl.multiple_of(held[v] % groups * piece // 16 * 16, 16), 16),
                pl.ds(pl.multiple_of((h * nic // 2 + held[v] // groups) * 128, 128), 128),
            ],
            tiles.at[v, h],
            load_sem.at[8 + 2 * v + h],
        )
        for v in range(2)
        for h in range(2)
    ]
    load_c = pltpu.make_async_copy(coef_ref, cbuf, load_sem.at[0])
    load_g = pltpu.make_async_copy(ints_ref, gbuf, load_sem.at[1])
    scalars = [
        pltpu.make_async_copy(pairs_hbm, pairs_ref, load_sem.at[4]),
        pltpu.make_async_copy(owner_hbm, owner_ref, load_sem.at[5]),
        pltpu.make_async_copy(slot_hbm, slot_ref, load_sem.at[6]),
    ]
    for copy in load_t:
        copy.start()
    for copy in scalars:
        copy.start()
    load_c.start()
    load_g.start()

    def remote(src, dst, stage, device):
        return pltpu.make_async_remote_copy(
            src_ref=src,
            dst_ref=dst,
            send_sem=send_sem.at[stage],
            recv_sem=recv_sem.at[stage],
            device_id=device,
            device_id_type=MESH,
        )

    def all_of(part, stage):
        return remote(part, part, stage, (a, sib))

    za, zb, wa, wb, ids_at, pa, pb, fs, xs = range(9)
    ds = xs + mp

    for v in range(2):
        for h in range(2):
            load_t[2 * v + h].wait()
            part = tiles[v, h]
            if piece < 16:
                part = jnp.where(held[v] % groups % 2 == 0, part[:, :piece], part[:, piece:])
            if v == 0:
                zbuf[h][own] = part
            else:
                zalt[h] = part

    for copy in scalars:
        copy.wait()

    row_at = lax.broadcasted_iota(I32, (8, width), 0)
    lane_at = lax.broadcasted_iota(I32, (8, width), 1)
    note = jnp.zeros((8, width), I32)
    for chunk in range(chunks):
        for h in range(2):
            for u in range(8):
                if places[chunk][u][h] is not None:
                    s, t = places[chunk][u][h]
                    j = s * (lmb - 1) + t - (1 if t > s else 0)
                    place = slot_ref[j] * na + owner_ref[j] + 1
                    here = (row_at == 2 * chunk + h) & ((lane_at == a * 16 + u) | (lane_at == a * 16 + 8 + u))
                    note = jnp.where(here, place, note)
    for s in range(lmb):
        for k in range(2):
            here = (row_at == 2 * chunks) & (lane_at == a * 16 + 2 * s + k)
            note = jnp.where(here, pairs_ref[4 * s + 2 + k], note)
    msgs[a] = note
    crossnote[...] = pltpu.roll(note, lax.rem(opposite + na - a, na) * 16, 1)

    pl.semaphore_wait(barrier, na + no - 2 + len(extra))

    def start_z(h, stage):
        for i in z_order:
            source = zbuf[h].at[own] if i % 2 == 0 else zalt.at[h]
            remote(source, zbuf[h].at[own], stage, (a, ((z + i) % nz) * 2 + c)).start()

    start_z(0, za)

    for there, orb, _, number in served_by:
        source = crossnote if number is opposite else msgs.at[a]
        remote(source, msgs.at[number], ids_at, (there, orb)).start()

    load_g.wait()
    height = bs * naux
    r_at = lax.broadcasted_iota(I32, (height, height), 0)
    c_at = lax.broadcasted_iota(I32, (height, height), 1)
    turn = (c_at == (r_at % bs) * naux + r_at // bs).astype(F32).astype(BF16)
    j = c_at - 2 * bs
    source = 2 * bs + (j // piece % 2) * bs + (j // (2 * piece)) * piece + j % piece
    order = (r_at == jnp.where(c_at < 2 * bs, c_at, source)).astype(F32).astype(BF16)
    for s in range(lmb):
        block = gbuf[4 * s : 4 * s + 4].reshape(4 * bs, height)
        turned = lax.dot_general(turn, block, (((1,), (1,)), ((), ())), preferred_element_type=F32).astype(BF16)
        gt[s] = jnp.dot(turned, order, preferred_element_type=F32).astype(BF16)

    def swap(h, z_stage, w_stage):
        all_of(zbuf[h].at[pl.ds(0, (nz - 1) * per)], z_stage).wait_recv()
        for i in range(nz):
            part = zbuf[h].at[pl.ds((2 * i + c) * per, per)]
            remote(part, part, w_stage, (a, sib)).start()

    start_z(1, zb)

    load_c.wait()
    for s in range(lmb):
        for k in range(2):
            near[s, pl.ds(k * bs, bs), :] = cbuf[lax.rem(pairs_ref[4 * s + k], per)]
    xbuf[...] = jnp.zeros_like(xbuf)

    all_of(msgs.at[pl.ds(0, na - 1)], ids_at).wait_recv()
    ids = msgs[0]
    for src in range(1, na):
        ids = ids + msgs[src]
    asked[...] = ids[2 * chunks : 2 * chunks + 1, :]
    to_scalar = pltpu.make_async_copy(asked, idsm, load_sem.at[3])
    to_scalar.start()
    swap(0, za, wa)
    to_scalar.wait()

    def pair(h, number, s):
        return jnp.concatenate([zbuf[h][idsm[0, number * 16 + 2 * s + k]] for k in range(2)], axis=0)

    def exchange(h, w_stage, p_stage):
        all_of(zbuf[h].at[pl.ds(0, nz * per)], w_stage).wait_recv()
        served = [(plane_at(dx, dy), plane_at(dx, dy), o) for dx, dy in near_by if abs(dx) + abs(dy) > 1]
        served += [
            (plane_at(shift - dx, shift - dy), plane_at(-dx, -dy), ((z - dz) % nz) * 2 + c) for dx, dy, dz in crossed
        ]
        served += [(plane_at(dx, dy), plane_at(dx, dy), o) for dx, dy in near_by if abs(dx) + abs(dy) == 1]
        for n, (number, asker, orb) in enumerate(served):
            for s in range(lmb):
                packed[h, n, s] = pair(h, number, s)
            remote(packed.at[h, n], far.at[h, tile], p_stage, (asker, orb)).start()
        for s in range(lmb):
            far[h, tile, s] = pair(h, a, s)

    exchange(0, wa, pa)
    swap(1, zb, wb)
    exchange(1, wb, pb)

    r_at = lax.broadcasted_iota(I32, (rows, width), 0) + 1
    l_at = (lax.broadcasted_iota(I32, (rows, width), 1) // 8) % 2
    for h in range(2):
        for tp in range(chunks):
            hit = r_at == ids[2 * tp + h : 2 * tp + h + 1, :]
            for m2 in range(2):
                onehot[pl.ds((m2 * 2 + h) * rows, rows), pl.ds(tp * width, width)] = (
                    jnp.where(hit & (l_at == m2), 1.0, 0.0).astype(BF16)
                )

    def multiply(h, p_stage):
        all_of(far.at[h, pl.ds(0, na - 1)], p_stage).wait_recv()
        wide = nocc // 2
        for s in range(lmb):
            there = [
                jnp.concatenate([far[h, i * groups + g, s] for g in range(groups)], axis=0) for i in range(nic // 2)
            ]
            there = jnp.concatenate(there, axis=1) if nic > 2 else there[0]
            block = jnp.concatenate([near[s, :, pl.ds(h * wide, wide)], there], axis=0)
            halfway = jnp.dot(gt[s], block, preferred_element_type=F32).astype(BF16)
            for p in range(naux):
                hcat[h, pl.ds(s * bs, bs), pl.ds(p * wide, wide)] = halfway[p * bs : (p + 1) * bs]
        whole = hcat[h]
        return lax.dot_general(whole, whole, (((1,), (1,)), ((), ())), preferred_element_type=F32)

    xhalf[...] = multiply(0, pa)
    products = xhalf[...] + multiply(1, pb)
    left = lax.broadcasted_iota(I32, (bs, 128), 1) < bs

    def block_half(place, h):
        s, t = place
        tile = products[s * bs : (s + 1) * bs, t // 2 * 128 : t // 2 * 128 + 128]
        return tile if t % 2 == h else pltpu.roll(tile, 64, 1)

    for chunk in range(chunks):
        for u in range(8):
            first, second = places[chunk][u]
            if first is not None:
                value = jnp.where(left, block_half(first, 0), block_half(second, 1))
                xbuf[chunk, pl.ds(u, bs, stride=8), :] = value

    def x_rows(e, q):
        at = pl.ds(pl.multiple_of((e * mp + q) * 16, 16), 16)
        return jnp.concatenate([xbuf[tp, at, :] for tp in range(chunks)], axis=1).astype(BF16)

    for q in range(mp):
        for n, (there, orb, e, number) in enumerate(served_by):
            xsend[q, n] = x_rows(e, q)
            remote(xsend.at[q, n], xrecv.at[q, number], xs + q, (there, orb)).start()
    for q in range(mp):
        xrecv[q, a] = x_rows(tile, q)

    low = lax.broadcasted_iota(I32, (rows, 128), 1) < 64

    def send_d(q):
        all_of(xrecv.at[q, pl.ds(0, na - 1)], xs + q).wait_recv()
        right = [xrecv[q, :, :, pl.ds(tp * 128, 128)].reshape(width, 128) for tp in range(chunks)]
        right = jnp.concatenate(right, axis=0)
        z00, z01, z10, z11 = [
            jnp.dot(onehot[pl.ds(block * rows, rows), :], right, preferred_element_type=F32) for block in range(4)
        ]
        first = z00 + pltpu.roll(z01, 64, 1)
        second = pltpu.roll(z10, 64, 1) + z11
        dsend[q] = jnp.where(low, first, second).astype(BF16).reshape(no, na, 128)
        for i in o_order:
            to = (o + i) % no
            remote(dsend.at[q, to], drecv.at[q, o], ds + q, (a, to)).start()
        drecv[q, o] = dsend[q, o]

    for q in range(mp):
        send_d(q)
    for q in range(mp):
        all_of(drecv.at[q, pl.ds(0, no - 1)], ds + q).wait_recv()
        for v in range(2):
            total = None
            for src in range(no):
                if src // 2 % 2 == v:
                    term = drecv[q, src].astype(F32)
                    total = term if total is None else total + term
            for r in range(na):
                fsend[r, :, pl.ds(v * el + q * 128, 128)] = total[r : r + 1, :]

    def send_f(i, _):
        to = plane_peer(i)
        remote(fsend.at[to], frecv.at[a], fs, (to, o)).start()
        return 0

    lax.fori_loop(0, na - 1, send_f, 0)
    frecv[a] = fsend[a]

    for h, (z_stage, w_stage, p_stage) in enumerate(((za, wa, pa), (zb, wb, pb))):
        all_of(zbuf[h].at[pl.ds(0, (nz - 1) * per)], z_stage).wait_send()
        all_of(zbuf[h].at[pl.ds(0, nz * per)], w_stage).wait_send()
        all_of(packed.at[h, pl.ds(0, na - 1)], p_stage).wait_send()
    all_of(msgs.at[pl.ds(0, na - 1)], ids_at).wait_send()
    for q in range(mp):
        all_of(xsend.at[q, pl.ds(0, na - 1)], xs + q).wait_send()
        all_of(dsend.at[q, pl.ds(0, no - 1)], ds + q).wait_send()
    all_of(frecv.at[pl.ds(0, na - 1)], fs).wait_recv()
    all_of(fsend.at[pl.ds(0, na - 1)], fs).wait_send()
    for e in range(na):
        other = (e // side + side // 2) % side * side + (e % side + side // 2) % side
        out_ref[:, pl.ds(e * el, el)] = frecv[e, :, pl.ds(0, el)] + frecv[other, :, pl.ds(el, el)]


def shards(integrals, coefficients, pair_list, partial_owner, partial_slot):
    na, no = lax.axis_size("aux"), lax.axis_size("orb")
    per, bs, nocc = coefficients.shape
    lmb = pair_list.shape[0] // 4
    naux = integrals.shape[2] // bs
    mp = bs // na // 2
    width = na * 16
    rows = na * no
    el = mp * 128
    chunks = (lmb - 2) // 2
    piece = bs * nocc // 256 // na
    dims = (na, no, lmb, bs, nocc, naux, per)
    dma = pltpu.SemaphoreType.DMA
    vmem = pltpu.VMEM
    any_spec = pl.BlockSpec(memory_space=pltpu.HBM)
    inputs = (integrals, coefficients, pair_list, partial_owner.reshape(-1), partial_slot)
    inputs = [pltpu.with_memory_space_constraint(value, pltpu.HBM) for value in inputs]
    return pl.pallas_call(
        functools.partial(kernel, dims),
        out_shape=pltpu.VMEM((1, bs * bs), F32),
        in_specs=[any_spec] * 5,
        out_specs=pl.BlockSpec(memory_space=pltpu.VMEM),
        scratch_shapes=[
            pltpu.SMEM(pair_list.shape, I32),
            pltpu.SMEM(partial_slot.shape, I32),
            pltpu.SMEM(partial_slot.shape, I32),
            vmem(integrals.shape, BF16),
            vmem(coefficients.shape, BF16),
            vmem((2, 2, per, 16, 128), BF16),
            vmem((2, per, piece, 128), BF16),
            vmem((no * per, piece, 128), BF16),
            vmem((no * per, piece, 128), BF16),
            vmem((na, 8, width), I32),
            vmem((8, width), I32),
            vmem((1, width), I32),
            pltpu.SMEM((1, width), I32),
            vmem((2, na, lmb, 2 * piece, 128), BF16),
            vmem((lmb, 2 * bs, nocc), BF16),
            vmem((2, na, lmb, 2 * piece, 128), BF16),
            vmem((lmb, bs * naux, 4 * bs), BF16),
            vmem((2, lmb * bs, naux * nocc // 2), BF16),
            vmem((lmb * bs, lmb * bs), F32),
            vmem((chunks, bs * 8, 128), F32),
            vmem((mp, na, 16, chunks * 128), BF16),
            vmem((mp, na, 16, chunks * 128), BF16),
            vmem((4 * rows, chunks * width), BF16),
            vmem((mp, no, na, 128), BF16),
            vmem((mp, no, na, 128), BF16),
            vmem((na, 1, 2 * el), F32),
            vmem((na, 1, 2 * el), F32),
            dma((12,)),
            dma((8 + 2 * mp,)),
            dma((8 + 2 * mp,)),
        ],
        compiler_params=pltpu.CompilerParams(
            collective_id=0, has_side_effects=True, vmem_limit_bytes=48 * 2**20
        ),
    )(*inputs)


def solution(mesh):
    in_specs = (
        P(("aux", "orb"), None, None),
        P("orb", None, None),
        P(("aux", "orb")),
        P(("aux", "orb"), None),
        P(("aux", "orb")),
    )
    out_specs = P(("aux", "orb"), None)
    return jax.shard_map(shards, mesh=mesh, in_specs=in_specs, out_specs=out_specs, check_vma=False)
```

```python
import functools
import math

import jax
import jax.numpy as jnp
from jax import lax
from jax.experimental import pallas as pl
from jax.experimental.pallas import tpu as pltpu
from jax.sharding import PartitionSpec as P

MESH = pl.DeviceIdType.MESH
F32, BF16, I32 = jnp.float32, jnp.bfloat16, jnp.int32


def holders(side):
    def distance(at):
        return sum(abs(d) for d in at)

    offsets = range(-((side - 1) // 2), side // 2 + 1)
    plane = [(dx, dy) for dx in offsets for dy in offsets if 0 < distance((dx, dy)) and 2 * distance((dx, dy)) <= side + 1]
    reach = [(dx, dy) for dx in offsets for dy in offsets if 2 * (side - distance((dx, dy))) > side + 1]
    return plane, [(dx, dy, 1 if dx + dy >= 0 else -1) for dx, dy in reach]


def block_places(lmb):
    chunks = (lmb - 2) // 2
    places = [[[None, None] for _ in range(8)] for _ in range(chunks)]
    for chunk in range(chunks):
        for s in range(lmb):
            for h in range(2):
                places[chunk][s][h] = (s, (s + 2 * chunk + 1 + h) % lmb)
    for s in range(lmb):
        row, h = divmod(s, 2)
        places[row // 2][lmb + row % 2][h] = (s, (s + lmb - 1) % lmb)
    return places


def kernel(
    dims,
    ints_ref,
    coef_ref,
    pairs_hbm,
    owner_hbm,
    slot_hbm,
    out_ref,
    pairs_ref,
    owner_ref,
    slot_ref,
    gbuf,
    cbuf,
    tiles,
    zalt,
    zbuf_a,
    zbuf_b,
    msgs,
    crossnote,
    asked,
    idsm,
    packed,
    near,
    far,
    gt,
    hcat,
    xhalf,
    xbuf,
    xsend,
    xrecv,
    onehot,
    dsend,
    drecv,
    fsend,
    frecv,
    load_sem,
    send_sem,
    recv_sem,
):
    na, no, lmb, bs, nocc, naux, per = dims
    side = math.isqrt(na)
    nz = no // 2
    nic = nocc // 128
    mp = bs // na // 2
    chunks = (lmb - 2) // 2
    places = block_places(lmb)
    width = na * 16
    rows = na * no
    el = mp * 128
    a = lax.axis_index("aux")
    o = lax.axis_index("orb")
    x, y = a // side, a % side
    z, c = o // 2, o % 2
    sib = o + 1 - 2 * c
    piece = bs * nic // 2 // na
    groups = bs // piece
    near_by, crossed = holders(side)

    def plane_at(dx, dy):
        return ((x + dx) % side) * side + (y + dy) % side

    turned = (side // 2) * (z % 2)
    tile = plane_at(turned, turned)
    shift = side // 2
    held = (tile, plane_at(shift - turned, shift - turned))
    opposite = plane_at(shift, shift)
    served_by = [(plane_at(dx, dy), o, plane_at(dx + turned, dy + turned), a) for dx, dy in near_by if abs(dx) + abs(dy) > 1]
    served_by += [
        (plane_at(dx, dy), ((z + dz) % nz) * 2 + c, plane_at(dx + shift - turned, dy + shift - turned), opposite)
        for dx, dy, dz in crossed
    ]
    served_by += [(plane_at(dx, dy), o, plane_at(dx + turned, dy + turned), a) for dx, dy in near_by if abs(dx) + abs(dy) == 1]
    own = pl.ds(o * per, per)
    zbuf = (zbuf_a, zbuf_b)

    def plane_peer(i):
        turn = na // 2 + side // 2
        j = jnp.where(i < na - turn, i + turn, i - (na - turn) + 1)
        return ((x + j // side) % side) * side + (y + j % side) % side

    z_order = sorted(range(1, nz), key=lambda i: -min(i, nz - i))
    o_order = sorted(range(1, no), key=lambda i: -min(i, no - i))

    barrier = pltpu.get_barrier_semaphore()
    for i in o_order:
        pl.semaphore_signal(barrier, inc=1, device_id=(a, (o + i) % no), device_id_type=MESH)

    def greet(i, _):
        pl.semaphore_signal(barrier, inc=1, device_id=(plane_peer(i), o), device_id_type=MESH)
        return 0

    for i in range(na - 1):
        greet(i, 0)
    extra = [at for at in crossed if at[:2] != (0, 0)]
    for dx, dy, dz in extra:
        there = (plane_at(dx, dy), ((z + dz) % nz) * 2 + c)
        pl.semaphore_signal(barrier, inc=1, device_id=there, device_id_type=MESH)

    load_t = [
        pltpu.make_async_copy(
            coef_ref.at[
                :,
                pl.ds(pl.multiple_of(held[v] % groups * piece // 16 * 16, 16), 16),
                pl.ds(pl.multiple_of((h * nic // 2 + held[v] // groups) * 128, 128), 128),
            ],
            tiles.at[v, h],
            load_sem.at[8 + 2 * v + h],
        )
        for v in range(2)
        for h in range(2)
    ]
    load_c = pltpu.make_async_copy(coef_ref, cbuf, load_sem.at[0])
    load_g = pltpu.make_async_copy(ints_ref, gbuf, load_sem.at[1])
    scalars = [
        pltpu.make_async_copy(pairs_hbm, pairs_ref, load_sem.at[4]),
        pltpu.make_async_copy(owner_hbm, owner_ref, load_sem.at[5]),
        pltpu.make_async_copy(slot_hbm, slot_ref, load_sem.at[6]),
    ]
    for copy in load_t:
        copy.start()
    for copy in scalars:
        copy.start()
    load_c.start()
    load_g.start()

    def remote(src, dst, stage, device):
        return pltpu.make_async_remote_copy(
            src_ref=src,
            dst_ref=dst,
            send_sem=send_sem.at[stage],
            recv_sem=recv_sem.at[stage],
            device_id=device,
            device_id_type=MESH,
        )

    def all_of(part, stage):
        return remote(part, part, stage, (a, sib))

    za, zb, wa, wb, ids_at, pa, pb, fs, xs = range(9)
    ds = xs + mp

    for v in range(2):
        for h in range(2):
            load_t[2 * v + h].wait()
            part = tiles[v, h]
            if piece < 16:
                part = jnp.where(held[v] % groups % 2 == 0, part[:, :piece], part[:, piece:])
            if v == 0:
                zbuf[h][own] = part
            else:
                zalt[h] = part

    pl.semaphore_wait(barrier, na + no - 2 + len(extra))

    def start_z(h, stage):
        for i in z_order:
            source = zbuf[h].at[own] if i % 2 == 0 else zalt.at[h]
            remote(source, zbuf[h].at[own], stage, (a, ((z + i) % nz) * 2 + c)).start()

    start_z(0, za)

    for copy in scalars:
        copy.wait()

    row_at = lax.broadcasted_iota(I32, (8, width), 0)
    lane_at = lax.broadcasted_iota(I32, (8, width), 1)
    note = jnp.zeros((8, width), I32)
    for chunk in range(chunks):
        for h in range(2):
            for u in range(8):
                if places[chunk][u][h] is not None:
                    s, t = places[chunk][u][h]
                    j = s * (lmb - 1) + t - (1 if t > s else 0)
                    place = slot_ref[j] * na + owner_ref[j] + 1
                    here = (row_at == 2 * chunk + h) & ((lane_at == a * 16 + u) | (lane_at == a * 16 + 8 + u))
                    note = jnp.where(here, place, note)
    for s in range(lmb):
        for k in range(2):
            here = (row_at == 2 * chunks) & (lane_at == a * 16 + 2 * s + k)
            note = jnp.where(here, pairs_ref[4 * s + 2 + k], note)
    msgs[a] = note
    crossnote[...] = pltpu.roll(note, lax.rem(opposite + na - a, na) * 16, 1)


    for there, orb, _, number in served_by:
        source = crossnote if number is opposite else msgs.at[a]
        remote(source, msgs.at[number], ids_at, (there, orb)).start()

    load_g.wait()
    height = bs * naux
    r_at = lax.broadcasted_iota(I32, (height, height), 0)
    c_at = lax.broadcasted_iota(I32, (height, height), 1)
    turn = (c_at == (r_at % bs) * naux + r_at // bs).astype(F32).astype(BF16)
    j = c_at - 2 * bs
    source = 2 * bs + (j // piece % 2) * bs + (j // (2 * piece)) * piece + j % piece
    order = (r_at == jnp.where(c_at < 2 * bs, c_at, source)).astype(F32).astype(BF16)
    for s in range(lmb):
        block = gbuf[4 * s : 4 * s + 4].reshape(4 * bs, height)
        turned = lax.dot_general(turn, block, (((1,), (1,)), ((), ())), preferred_element_type=F32).astype(BF16)
        gt[s] = jnp.dot(turned, order, preferred_element_type=F32).astype(BF16)

    def swap(h, z_stage, w_stage):
        all_of(zbuf[h].at[pl.ds(0, (nz - 1) * per)], z_stage).wait_recv()
        for i in range(nz):
            part = zbuf[h].at[pl.ds((2 * i + c) * per, per)]
            remote(part, part, w_stage, (a, sib)).start()

    start_z(1, zb)

    load_c.wait()
    for s in range(lmb):
        for k in range(2):
            near[s, pl.ds(k * bs, bs), :] = cbuf[lax.rem(pairs_ref[4 * s + k], per)]
    xbuf[...] = jnp.zeros_like(xbuf)

    all_of(msgs.at[pl.ds(0, na - 1)], ids_at).wait_recv()
    ids = msgs[0]
    for src in range(1, na):
        ids = ids + msgs[src]
    asked[...] = ids[2 * chunks : 2 * chunks + 1, :]
    to_scalar = pltpu.make_async_copy(asked, idsm, load_sem.at[3])
    to_scalar.start()
    swap(0, za, wa)
    to_scalar.wait()

    def pair(h, number, s):
        return jnp.concatenate([zbuf[h][idsm[0, number * 16 + 2 * s + k]] for k in range(2)], axis=0)

    def exchange(h, w_stage, p_stage):
        all_of(zbuf[h].at[pl.ds(0, nz * per)], w_stage).wait_recv()
        served = [(plane_at(dx, dy), plane_at(dx, dy), o) for dx, dy in near_by if abs(dx) + abs(dy) > 1]
        served += [
            (plane_at(shift - dx, shift - dy), plane_at(-dx, -dy), ((z - dz) % nz) * 2 + c) for dx, dy, dz in crossed
        ]
        served += [(plane_at(dx, dy), plane_at(dx, dy), o) for dx, dy in near_by if abs(dx) + abs(dy) == 1]
        for n, (number, asker, orb) in enumerate(served):
            for s in range(lmb):
                packed[h, n, s] = pair(h, number, s)
            remote(packed.at[h, n], far.at[h, tile], p_stage, (asker, orb)).start()
        for s in range(lmb):
            far[h, tile, s] = pair(h, a, s)

    exchange(0, wa, pa)
    swap(1, zb, wb)
    exchange(1, wb, pb)

    r_at = lax.broadcasted_iota(I32, (rows, width), 0) + 1
    l_at = (lax.broadcasted_iota(I32, (rows, width), 1) // 8) % 2
    for h in range(2):
        for tp in range(chunks):
            hit = r_at == ids[2 * tp + h : 2 * tp + h + 1, :]
            for m2 in range(2):
                onehot[pl.ds((m2 * 2 + h) * rows, rows), pl.ds(tp * width, width)] = (
                    jnp.where(hit & (l_at == m2), 1.0, 0.0).astype(BF16)
                )

    def multiply(h, p_stage):
        all_of(far.at[h, pl.ds(0, na - 1)], p_stage).wait_recv()
        wide = nocc // 2
        for s in range(lmb):
            there = [
                jnp.concatenate([far[h, i * groups + g, s] for g in range(groups)], axis=0) for i in range(nic // 2)
            ]
            there = jnp.concatenate(there, axis=1) if nic > 2 else there[0]
            block = jnp.concatenate([near[s, :, pl.ds(h * wide, wide)], there], axis=0)
            halfway = jnp.dot(gt[s], block, preferred_element_type=F32).astype(BF16)
            for p in range(naux):
                hcat[h, pl.ds(s * bs, bs), pl.ds(p * wide, wide)] = halfway[p * bs : (p + 1) * bs]
        whole = hcat[h]
        return lax.dot_general(whole, whole, (((1,), (1,)), ((), ())), preferred_element_type=F32)

    xhalf[...] = multiply(0, pa)
    products = xhalf[...] + multiply(1, pb)
    left = lax.broadcasted_iota(I32, (bs, 128), 1) < bs

    def block_half(place, h):
        s, t = place
        tile = products[s * bs : (s + 1) * bs, t // 2 * 128 : t // 2 * 128 + 128]
        return tile if t % 2 == h else pltpu.roll(tile, 64, 1)

    for chunk in range(chunks):
        for u in range(8):
            first, second = places[chunk][u]
            if first is not None:
                value = jnp.where(left, block_half(first, 0), block_half(second, 1))
                xbuf[chunk, pl.ds(u, bs, stride=8), :] = value

    def x_rows(e, q):
        at = pl.ds(pl.multiple_of((e * mp + q) * 16, 16), 16)
        return jnp.concatenate([xbuf[tp, at, :] for tp in range(chunks)], axis=1).astype(BF16)

    for q in range(mp):
        for n, (there, orb, e, number) in enumerate(served_by):
            xsend[q, n] = x_rows(e, q)
            remote(xsend.at[q, n], xrecv.at[q, number], xs + q, (there, orb)).start()
    for q in range(mp):
        xrecv[q, a] = x_rows(tile, q)

    low = lax.broadcasted_iota(I32, (rows, 128), 1) < 64

    def send_d(q):
        all_of(xrecv.at[q, pl.ds(0, na - 1)], xs + q).wait_recv()
        right = [xrecv[q, :, :, pl.ds(tp * 128, 128)].reshape(width, 128) for tp in range(chunks)]
        right = jnp.concatenate(right, axis=0)
        z00, z01, z10, z11 = [
            jnp.dot(onehot[pl.ds(block * rows, rows), :], right, preferred_element_type=F32) for block in range(4)
        ]
        first = z00 + pltpu.roll(z01, 64, 1)
        second = pltpu.roll(z10, 64, 1) + z11
        dsend[q] = jnp.where(low, first, second).astype(BF16).reshape(no, na, 128)
        for i in o_order:
            to = (o + i) % no
            remote(dsend.at[q, to], drecv.at[q, o], ds + q, (a, to)).start()
        drecv[q, o] = dsend[q, o]

    for q in range(mp):
        send_d(q)
    for q in range(mp):
        all_of(drecv.at[q, pl.ds(0, no - 1)], ds + q).wait_recv()
        for v in range(2):
            total = None
            for src in range(no):
                if src // 2 % 2 == v:
                    term = drecv[q, src].astype(F32)
                    total = term if total is None else total + term
            for r in range(na):
                fsend[r, :, pl.ds(v * el + q * 128, 128)] = total[r : r + 1, :]

    def send_f(i, _):
        to = plane_peer(i)
        remote(fsend.at[to], frecv.at[a], fs, (to, o)).start()
        return 0

    lax.fori_loop(0, na - 1, send_f, 0)
    frecv[a] = fsend[a]

    for h, (z_stage, w_stage, p_stage) in enumerate(((za, wa, pa), (zb, wb, pb))):
        all_of(zbuf[h].at[pl.ds(0, (nz - 1) * per)], z_stage).wait_send()
        all_of(zbuf[h].at[pl.ds(0, nz * per)], w_stage).wait_send()
        all_of(packed.at[h, pl.ds(0, na - 1)], p_stage).wait_send()
    all_of(msgs.at[pl.ds(0, na - 1)], ids_at).wait_send()
    for q in range(mp):
        all_of(xsend.at[q, pl.ds(0, na - 1)], xs + q).wait_send()
        all_of(dsend.at[q, pl.ds(0, no - 1)], ds + q).wait_send()
    all_of(frecv.at[pl.ds(0, na - 1)], fs).wait_recv()
    all_of(fsend.at[pl.ds(0, na - 1)], fs).wait_send()
    for e in range(na):
        other = (e // side + side // 2) % side * side + (e % side + side // 2) % side
        out_ref[:, pl.ds(e * el, el)] = frecv[e, :, pl.ds(0, el)] + frecv[other, :, pl.ds(el, el)]


def shards(integrals, coefficients, pair_list, partial_owner, partial_slot):
    na, no = lax.axis_size("aux"), lax.axis_size("orb")
    per, bs, nocc = coefficients.shape
    lmb = pair_list.shape[0] // 4
    naux = integrals.shape[2] // bs
    mp = bs // na // 2
    width = na * 16
    rows = na * no
    el = mp * 128
    chunks = (lmb - 2) // 2
    piece = bs * nocc // 256 // na
    dims = (na, no, lmb, bs, nocc, naux, per)
    dma = pltpu.SemaphoreType.DMA
    vmem = pltpu.VMEM
    any_spec = pl.BlockSpec(memory_space=pltpu.HBM)
    inputs = (integrals, coefficients, pair_list, partial_owner.reshape(-1), partial_slot)
    inputs = [pltpu.with_memory_space_constraint(value, pltpu.HBM) for value in inputs]
    return pl.pallas_call(
        functools.partial(kernel, dims),
        out_shape=pltpu.VMEM((1, bs * bs), F32),
        in_specs=[any_spec] * 5,
        out_specs=pl.BlockSpec(memory_space=pltpu.VMEM),
        scratch_shapes=[
            pltpu.SMEM(pair_list.shape, I32),
            pltpu.SMEM(partial_slot.shape, I32),
            pltpu.SMEM(partial_slot.shape, I32),
            vmem(integrals.shape, BF16),
            vmem(coefficients.shape, BF16),
            vmem((2, 2, per, 16, 128), BF16),
            vmem((2, per, piece, 128), BF16),
            vmem((no * per, piece, 128), BF16),
            vmem((no * per, piece, 128), BF16),
            vmem((na, 8, width), I32),
            vmem((8, width), I32),
            vmem((1, width), I32),
            pltpu.SMEM((1, width), I32),
            vmem((2, na, lmb, 2 * piece, 128), BF16),
            vmem((lmb, 2 * bs, nocc), BF16),
            vmem((2, na, lmb, 2 * piece, 128), BF16),
            vmem((lmb, bs * naux, 4 * bs), BF16),
            vmem((2, lmb * bs, naux * nocc // 2), BF16),
            vmem((lmb * bs, lmb * bs), F32),
            vmem((chunks, bs * 8, 128), F32),
            vmem((mp, na, 16, chunks * 128), BF16),
            vmem((mp, na, 16, chunks * 128), BF16),
            vmem((4 * rows, chunks * width), BF16),
            vmem((mp, no, na, 128), BF16),
            vmem((mp, no, na, 128), BF16),
            vmem((na, 1, 2 * el), F32),
            vmem((na, 1, 2 * el), F32),
            dma((12,)),
            dma((8 + 2 * mp,)),
            dma((8 + 2 * mp,)),
        ],
        compiler_params=pltpu.CompilerParams(
            collective_id=0, has_side_effects=True, vmem_limit_bytes=48 * 2**20
        ),
    )(*inputs)


def solution(mesh):
    in_specs = (
        P(("aux", "orb"), None, None),
        P("orb", None, None),
        P(("aux", "orb")),
        P(("aux", "orb"), None),
        P(("aux", "orb")),
    )
    out_specs = P(("aux", "orb"), None)
    return jax.shard_map(shards, mesh=mesh, in_specs=in_specs, out_specs=out_specs, check_vma=False)
```

```python
import functools
import math

import jax
import jax.numpy as jnp
from jax import lax
from jax.experimental import pallas as pl
from jax.experimental.pallas import tpu as pltpu
from jax.sharding import PartitionSpec as P

MESH = pl.DeviceIdType.MESH
F32, BF16, I32 = jnp.float32, jnp.bfloat16, jnp.int32


def holders(side):
    def distance(at):
        return sum(abs(d) for d in at)

    offsets = range(-((side - 1) // 2), side // 2 + 1)
    plane = [(dx, dy) for dx in offsets for dy in offsets if 0 < distance((dx, dy)) and 2 * distance((dx, dy)) <= side + 1]
    reach = [(dx, dy) for dx in offsets for dy in offsets if 2 * (side - distance((dx, dy))) > side + 1]
    return plane, [(dx, dy, 1 if dx + dy >= 0 else -1) for dx, dy in reach]


def block_places(lmb):
    chunks = (lmb - 2) // 2
    places = [[[None, None] for _ in range(8)] for _ in range(chunks)]
    for chunk in range(chunks):
        for s in range(lmb):
            for h in range(2):
                places[chunk][s][h] = (s, (s + 2 * chunk + 1 + h) % lmb)
    for s in range(lmb):
        row, h = divmod(s, 2)
        places[row // 2][lmb + row % 2][h] = (s, (s + lmb - 1) % lmb)
    return places


def kernel(
    dims,
    ints_ref,
    coef_ref,
    pairs_hbm,
    owner_hbm,
    slot_hbm,
    out_ref,
    pairs_ref,
    owner_ref,
    slot_ref,
    gbuf,
    cbuf,
    tiles,
    zalt,
    zbuf_a,
    zbuf_b,
    msgs,
    crossnote,
    asked,
    idsm,
    packed,
    near,
    far,
    gt,
    hcat,
    xhalf,
    xbuf,
    xsend,
    xrecv,
    onehot,
    dsend,
    drecv,
    fsend,
    frecv,
    load_sem,
    send_sem,
    recv_sem,
):
    na, no, lmb, bs, nocc, naux, per = dims
    side = math.isqrt(na)
    nz = no // 2
    nic = nocc // 128
    mp = bs // na // 2
    chunks = (lmb - 2) // 2
    places = block_places(lmb)
    width = na * 16
    rows = na * no
    el = mp * 128
    a = lax.axis_index("aux")
    o = lax.axis_index("orb")
    x, y = a // side, a % side
    z, c = o // 2, o % 2
    sib = o + 1 - 2 * c
    piece = bs * nic // 2 // na
    groups = bs // piece
    near_by, crossed = holders(side)

    def plane_at(dx, dy):
        return ((x + dx) % side) * side + (y + dy) % side

    turned = (side // 2) * (z % 2)
    tile = plane_at(turned, turned)
    shift = side // 2
    held = (tile, plane_at(shift - turned, shift - turned))
    opposite = plane_at(shift, shift)
    served_by = [(plane_at(dx, dy), o, plane_at(dx + turned, dy + turned), a) for dx, dy in near_by if abs(dx) + abs(dy) > 1]
    served_by += [
        (plane_at(dx, dy), ((z + dz) % nz) * 2 + c, plane_at(dx + shift - turned, dy + shift - turned), opposite)
        for dx, dy, dz in crossed
    ]
    served_by += [(plane_at(dx, dy), o, plane_at(dx + turned, dy + turned), a) for dx, dy in near_by if abs(dx) + abs(dy) == 1]
    own = pl.ds(o * per, per)
    zbuf = (zbuf_a, zbuf_b)

    def plane_peer(i):
        turn = na // 2 + side // 2
        j = jnp.where(i < na - turn, i + turn, i - (na - turn) + 1)
        return ((x + j // side) % side) * side + (y + j % side) % side

    z_order = sorted(range(1, nz), key=lambda i: -min(i, nz - i))
    o_order = sorted(range(1, no), key=lambda i: -min(i, no - i))

    barrier = pltpu.get_barrier_semaphore()
    for i in o_order:
        pl.semaphore_signal(barrier, inc=1, device_id=(a, (o + i) % no), device_id_type=MESH)

    def greet(i, _):
        pl.semaphore_signal(barrier, inc=1, device_id=(plane_peer(i), o), device_id_type=MESH)
        return 0

    for i in range(na - 1):
        greet(i, 0)
    extra = [at for at in crossed if at[:2] != (0, 0)]
    for dx, dy, dz in extra:
        there = (plane_at(dx, dy), ((z + dz) % nz) * 2 + c)
        pl.semaphore_signal(barrier, inc=1, device_id=there, device_id_type=MESH)

    load_t = [
        pltpu.make_async_copy(
            coef_ref.at[
                :,
                pl.ds(pl.multiple_of(held[v] % groups * piece // 16 * 16, 16), 16),
                pl.ds(pl.multiple_of((h * nic // 2 + held[v] // groups) * 128, 128), 128),
            ],
            tiles.at[v, h],
            load_sem.at[(2, 7, 8, 9)[2 * v + h]],
        )
        for v in range(2)
        for h in range(2)
    ]
    load_c = pltpu.make_async_copy(coef_ref, cbuf, load_sem.at[0])
    load_g = pltpu.make_async_copy(ints_ref, gbuf, load_sem.at[1])
    scalars = [
        pltpu.make_async_copy(pairs_hbm, pairs_ref, load_sem.at[4]),
        pltpu.make_async_copy(owner_hbm, owner_ref, load_sem.at[5]),
        pltpu.make_async_copy(slot_hbm, slot_ref, load_sem.at[6]),
    ]
    for copy in load_t:
        copy.start()
    for copy in scalars:
        copy.start()
    load_c.start()
    load_g.start()

    def remote(src, dst, stage, device):
        return pltpu.make_async_remote_copy(
            src_ref=src,
            dst_ref=dst,
            send_sem=send_sem.at[stage],
            recv_sem=recv_sem.at[stage],
            device_id=device,
            device_id_type=MESH,
        )

    def all_of(part, stage):
        return remote(part, part, stage, (a, sib))

    za, zb, wa, wb, ids_at, pa, pb, fs, xs = range(9)
    ds = xs + mp

    for v in range(2):
        for h in range(2):
            load_t[2 * v + h].wait()
            part = tiles[v, h]
            if piece < 16:
                part = jnp.where(held[v] % groups % 2 == 0, part[:, :piece], part[:, piece:])
            if v == 0:
                zbuf[h][own] = part
            else:
                zalt[h] = part

    pl.semaphore_wait(barrier, na + no - 2 + len(extra))

    def start_z(h, stage):
        for i in z_order:
            source = zbuf[h].at[own] if i % 2 == 0 else zalt.at[h]
            remote(source, zbuf[h].at[own], stage, (a, ((z + i) % nz) * 2 + c)).start()

    start_z(0, za)

    for copy in scalars:
        copy.wait()

    row_at = lax.broadcasted_iota(I32, (8, width), 0)
    lane_at = lax.broadcasted_iota(I32, (8, width), 1)
    note = jnp.zeros((8, width), I32)
    for chunk in range(chunks):
        for h in range(2):
            for u in range(8):
                if places[chunk][u][h] is not None:
                    s, t = places[chunk][u][h]
                    j = s * (lmb - 1) + t - (1 if t > s else 0)
                    place = slot_ref[j] * na + owner_ref[j] + 1
                    here = (row_at == 2 * chunk + h) & ((lane_at == a * 16 + u) | (lane_at == a * 16 + 8 + u))
                    note = jnp.where(here, place, note)
    for s in range(lmb):
        for k in range(2):
            here = (row_at == 2 * chunks) & (lane_at == a * 16 + 2 * s + k)
            note = jnp.where(here, pairs_ref[4 * s + 2 + k], note)
    msgs[a] = note
    crossnote[...] = pltpu.roll(note, lax.rem(opposite + na - a, na) * 16, 1)


    for there, orb, _, number in served_by:
        source = crossnote if number is opposite else msgs.at[a]
        remote(source, msgs.at[number], ids_at, (there, orb)).start()

    load_g.wait()
    height = bs * naux
    r_at = lax.broadcasted_iota(I32, (height, height), 0)
    c_at = lax.broadcasted_iota(I32, (height, height), 1)
    turn = (c_at == (r_at % bs) * naux + r_at // bs).astype(F32).astype(BF16)
    j = c_at - 2 * bs
    source = 2 * bs + (j // piece % 2) * bs + (j // (2 * piece)) * piece + j % piece
    order = (r_at == jnp.where(c_at < 2 * bs, c_at, source)).astype(F32).astype(BF16)
    for s in range(lmb):
        block = gbuf[4 * s : 4 * s + 4].reshape(4 * bs, height)
        turned = lax.dot_general(turn, block, (((1,), (1,)), ((), ())), preferred_element_type=F32).astype(BF16)
        gt[s] = jnp.dot(turned, order, preferred_element_type=F32).astype(BF16)

    def swap(h, z_stage, w_stage):
        all_of(zbuf[h].at[pl.ds(0, (nz - 1) * per)], z_stage).wait_recv()
        for i in range(nz):
            part = zbuf[h].at[pl.ds((2 * i + c) * per, per)]
            remote(part, part, w_stage, (a, sib)).start()

    start_z(1, zb)

    load_c.wait()
    for s in range(lmb):
        for k in range(2):
            near[s, pl.ds(k * bs, bs), :] = cbuf[lax.rem(pairs_ref[4 * s + k], per)]
    xbuf[...] = jnp.zeros_like(xbuf)

    all_of(msgs.at[pl.ds(0, na - 1)], ids_at).wait_recv()
    ids = msgs[0]
    for src in range(1, na):
        ids = ids + msgs[src]
    asked[...] = ids[2 * chunks : 2 * chunks + 1, :]
    to_scalar = pltpu.make_async_copy(asked, idsm, load_sem.at[3])
    to_scalar.start()
    swap(0, za, wa)
    to_scalar.wait()

    def pair(h, number, s):
        return jnp.concatenate([zbuf[h][idsm[0, number * 16 + 2 * s + k]] for k in range(2)], axis=0)

    def exchange(h, w_stage, p_stage):
        all_of(zbuf[h].at[pl.ds(0, nz * per)], w_stage).wait_recv()
        served = [
            (plane_at(shift - dx, shift - dy), plane_at(-dx, -dy), ((z - dz) % nz) * 2 + c) for dx, dy, dz in crossed
        ]
        served += [(plane_at(dx, dy), plane_at(dx, dy), o) for dx, dy in near_by if abs(dx) + abs(dy) > 1]
        served += [(plane_at(dx, dy), plane_at(dx, dy), o) for dx, dy in near_by if abs(dx) + abs(dy) == 1]
        for n, (number, asker, orb) in enumerate(served):
            for s in range(lmb):
                packed[h, n, s] = pair(h, number, s)
            remote(packed.at[h, n], far.at[h, tile], p_stage, (asker, orb)).start()
        for s in range(lmb):
            far[h, tile, s] = pair(h, a, s)

    exchange(0, wa, pa)
    swap(1, zb, wb)
    exchange(1, wb, pb)

    r_at = lax.broadcasted_iota(I32, (rows, width), 0) + 1
    l_at = (lax.broadcasted_iota(I32, (rows, width), 1) // 8) % 2
    for h in range(2):
        for tp in range(chunks):
            hit = r_at == ids[2 * tp + h : 2 * tp + h + 1, :]
            for m2 in range(2):
                onehot[pl.ds((m2 * 2 + h) * rows, rows), pl.ds(tp * width, width)] = (
                    jnp.where(hit & (l_at == m2), 1.0, 0.0).astype(BF16)
                )

    def multiply(h, p_stage):
        all_of(far.at[h, pl.ds(0, na - 1)], p_stage).wait_recv()
        wide = nocc // 2
        for s in range(lmb):
            there = [
                jnp.concatenate([far[h, i * groups + g, s] for g in range(groups)], axis=0) for i in range(nic // 2)
            ]
            there = jnp.concatenate(there, axis=1) if nic > 2 else there[0]
            block = jnp.concatenate([near[s, :, pl.ds(h * wide, wide)], there], axis=0)
            halfway = jnp.dot(gt[s], block, preferred_element_type=F32).astype(BF16)
            for p in range(naux):
                hcat[h, pl.ds(s * bs, bs), pl.ds(p * wide, wide)] = halfway[p * bs : (p + 1) * bs]
        whole = hcat[h]
        return lax.dot_general(whole, whole, (((1,), (1,)), ((), ())), preferred_element_type=F32)

    xhalf[...] = multiply(0, pa)
    products = xhalf[...] + multiply(1, pb)
    left = lax.broadcasted_iota(I32, (bs, 128), 1) < bs

    def block_half(place, h):
        s, t = place
        tile = products[s * bs : (s + 1) * bs, t // 2 * 128 : t // 2 * 128 + 128]
        return tile if t % 2 == h else pltpu.roll(tile, 64, 1)

    for chunk in range(chunks):
        for u in range(8):
            first, second = places[chunk][u]
            if first is not None:
                value = jnp.where(left, block_half(first, 0), block_half(second, 1))
                xbuf[chunk, pl.ds(u, bs, stride=8), :] = value

    def x_rows(e, q):
        at = pl.ds(pl.multiple_of((e * mp + q) * 16, 16), 16)
        return jnp.concatenate([xbuf[tp, at, :] for tp in range(chunks)], axis=1).astype(BF16)

    for q in range(mp):
        for n, (there, orb, e, number) in enumerate(served_by):
            xsend[q, n] = x_rows(e, q)
            remote(xsend.at[q, n], xrecv.at[q, number], xs + q, (there, orb)).start()
    for q in range(mp):
        xrecv[q, a] = x_rows(tile, q)

    low = lax.broadcasted_iota(I32, (rows, 128), 1) < 64

    def send_d(q):
        all_of(xrecv.at[q, pl.ds(0, na - 1)], xs + q).wait_recv()
        right = [xrecv[q, :, :, pl.ds(tp * 128, 128)].reshape(width, 128) for tp in range(chunks)]
        right = jnp.concatenate(right, axis=0)
        z00, z01, z10, z11 = [
            jnp.dot(onehot[pl.ds(block * rows, rows), :], right, preferred_element_type=F32) for block in range(4)
        ]
        first = z00 + pltpu.roll(z01, 64, 1)
        second = pltpu.roll(z10, 64, 1) + z11
        dsend[q] = jnp.where(low, first, second).astype(BF16).reshape(no, na, 128)
        for i in o_order:
            to = (o + i) % no
            remote(dsend.at[q, to], drecv.at[q, o], ds + q, (a, to)).start()
        drecv[q, o] = dsend[q, o]

    for q in range(mp):
        send_d(q)
    for q in range(mp):
        all_of(drecv.at[q, pl.ds(0, no - 1)], ds + q).wait_recv()
        for v in range(2):
            total = None
            for src in range(no):
                if src // 2 % 2 == v:
                    term = drecv[q, src].astype(F32)
                    total = term if total is None else total + term
            for r in range(na):
                fsend[r, :, pl.ds(v * el + q * 128, 128)] = total[r : r + 1, :]

    def send_f(i, _):
        to = plane_peer(i)
        remote(fsend.at[to], frecv.at[a], fs, (to, o)).start()
        return 0

    lax.fori_loop(0, na - 1, send_f, 0)
    frecv[a] = fsend[a]

    for h, (z_stage, w_stage, p_stage) in enumerate(((za, wa, pa), (zb, wb, pb))):
        all_of(zbuf[h].at[pl.ds(0, (nz - 1) * per)], z_stage).wait_send()
        all_of(zbuf[h].at[pl.ds(0, nz * per)], w_stage).wait_send()
        all_of(packed.at[h, pl.ds(0, na - 1)], p_stage).wait_send()
    all_of(msgs.at[pl.ds(0, na - 1)], ids_at).wait_send()
    for q in range(mp):
        all_of(xsend.at[q, pl.ds(0, na - 1)], xs + q).wait_send()
        all_of(dsend.at[q, pl.ds(0, no - 1)], ds + q).wait_send()
    all_of(frecv.at[pl.ds(0, na - 1)], fs).wait_recv()
    all_of(fsend.at[pl.ds(0, na - 1)], fs).wait_send()
    for e in range(na):
        other = (e // side + side // 2) % side * side + (e % side + side // 2) % side
        out_ref[:, pl.ds(e * el, el)] = frecv[e, :, pl.ds(0, el)] + frecv[other, :, pl.ds(el, el)]


def shards(integrals, coefficients, pair_list, partial_owner, partial_slot):
    na, no = lax.axis_size("aux"), lax.axis_size("orb")
    per, bs, nocc = coefficients.shape
    lmb = pair_list.shape[0] // 4
    naux = integrals.shape[2] // bs
    mp = bs // na // 2
    width = na * 16
    rows = na * no
    el = mp * 128
    chunks = (lmb - 2) // 2
    piece = bs * nocc // 256 // na
    dims = (na, no, lmb, bs, nocc, naux, per)
    dma = pltpu.SemaphoreType.DMA
    vmem = pltpu.VMEM
    any_spec = pl.BlockSpec(memory_space=pltpu.HBM)
    inputs = (integrals, coefficients, pair_list, partial_owner.reshape(-1), partial_slot)
    inputs = [pltpu.with_memory_space_constraint(value, pltpu.HBM) for value in inputs]
    return pl.pallas_call(
        functools.partial(kernel, dims),
        out_shape=pltpu.VMEM((1, bs * bs), F32),
        in_specs=[any_spec] * 5,
        out_specs=pl.BlockSpec(memory_space=pltpu.VMEM),
        scratch_shapes=[
            pltpu.SMEM(pair_list.shape, I32),
            pltpu.SMEM(partial_slot.shape, I32),
            pltpu.SMEM(partial_slot.shape, I32),
            vmem(integrals.shape, BF16),
            vmem(coefficients.shape, BF16),
            vmem((2, 2, per, 16, 128), BF16),
            vmem((2, per, piece, 128), BF16),
            vmem((no * per, piece, 128), BF16),
            vmem((no * per, piece, 128), BF16),
            vmem((na, 8, width), I32),
            vmem((8, width), I32),
            vmem((1, width), I32),
            pltpu.SMEM((1, width), I32),
            vmem((2, na, lmb, 2 * piece, 128), BF16),
            vmem((lmb, 2 * bs, nocc), BF16),
            vmem((2, na, lmb, 2 * piece, 128), BF16),
            vmem((lmb, bs * naux, 4 * bs), BF16),
            vmem((2, lmb * bs, naux * nocc // 2), BF16),
            vmem((lmb * bs, lmb * bs), F32),
            vmem((chunks, bs * 8, 128), F32),
            vmem((mp, na, 16, chunks * 128), BF16),
            vmem((mp, na, 16, chunks * 128), BF16),
            vmem((4 * rows, chunks * width), BF16),
            vmem((mp, no, na, 128), BF16),
            vmem((mp, no, na, 128), BF16),
            vmem((na, 1, 2 * el), F32),
            vmem((na, 1, 2 * el), F32),
            dma((10,)),
            dma((8 + 2 * mp,)),
            dma((8 + 2 * mp,)),
        ],
        compiler_params=pltpu.CompilerParams(
            collective_id=0, has_side_effects=True, vmem_limit_bytes=48 * 2**20
        ),
    )(*inputs)


def solution(mesh):
    in_specs = (
        P(("aux", "orb"), None, None),
        P("orb", None, None),
        P(("aux", "orb")),
        P(("aux", "orb"), None),
        P(("aux", "orb")),
    )
    out_specs = P(("aux", "orb"), None)
    return jax.shard_map(shards, mesh=mesh, in_specs=in_specs, out_specs=out_specs, check_vma=False)
```
